512 devices in a mesh: ctx: 64 (over z_lo, y, core), head: 8 (over x, z_hi).
Axes of the slice: x: 4, y: 4, z: 16 (z_hi: 2, z_lo: 8; z = z_hi * 8 + z_lo), core: 2. Of those that a mesh axis runs over, the one named last changes fastest.
Arguments:
- queries: bfloat16 [8192, 6144], P('ctx', 'head'), may hold values from -5 to 5
- keys: bfloat16 [8192, 1024], P('ctx', 'head'), may hold values from -5 to 5
- values: bfloat16 [8192, 1024], P('ctx', 'head'), may hold values from -6 to 6
- cotangent: bfloat16 [8192, 6144], P('ctx', 'head'), may hold values from -6 to 6
- seg_lengths: int32 [128], replicated, may hold values from 1 to 1024, 8192 in all
- seg_return: float32 [128], replicated, may hold values from -1 to 1
- owner_slot: int32 [8192], P('ctx'), may hold values from 0 to 8191, each once
- ref_term: float32 [8192], P(('ctx', 'head')), may hold values from -1 to 1
Outputs:
- grad_queries: bfloat16 [8192, 6144], P('ctx', 'head')
- grad_keys: bfloat16 [8192, 1024], P('ctx', 'head')
- grad_values: bfloat16 [8192, 1024], P('ctx', 'head')
The draws below stay inside these ranges and needn't reach their ends.
Inputs may be any that keep to these rules, and one draw needn't show every extreme that they name: `seg_lengths`: the lengths sum to 8192; the largest is exactly 1024. `owner_slot`: every value appears exactly once.
All inputs are finite; a program needn't handle non-finite values.
Results may differ from the reference program's by a relative error of at most 0.012.
Values may be sent and summed in bfloat16 or wider, within the bound.
No kernel may reach another device: no remote copies, remote signals or barrier semaphores. Data moves between devices by JAX's collectives and lax.ppermute only.
A program may use at most 64 MiB of HBM per device.

```python
import math
import jax
import jax.numpy as jnp
import numpy as np
from jax import lax

E = 128
GROUP = 6
TOK_DEV = 128
SEGS = 128
KV = 8
HQ = 48
TOKENS = 8192
SEG_MOST = 1024
N_CTX = 64


def draw_queries(key, part):
    key = jax.random.fold_in(key, 11)
    result = jnp.clip(jax.random.normal(key, (TOKENS, KV, GROUP, E), jnp.float32), -4.0, 4.0)
    return result.reshape(TOKENS, KV * GROUP * E).astype(jnp.bfloat16)


def draw_keys(key, part):
    key = jax.random.fold_in(key, 12)
    result = jnp.clip(jax.random.normal(key, (TOKENS, KV, E), jnp.float32), -4.0, 4.0)
    return result.reshape(TOKENS, KV * E).astype(jnp.bfloat16)


def level_of(own_key, extent, shards, low, top_value):
    factor_of, own = 1.0, jax.random.fold_in(own_key, 6)
    for dim, shards_of in shards:
        draws = jnp.exp(jax.random.uniform(jax.random.fold_in(own, dim), (shards_of,), jnp.float32, low / len(shards), top_value / len(shards)))
        factor_of = factor_of * jnp.repeat(draws, extent[dim] // shards_of).reshape([-1 if axis == dim else 1 for axis in range(len(extent))])
    return factor_of


def length_profile(number_of, total, limit, skew):
    portions = [(1 << 20) // math.isqrt(rank ** skew) + 1 for rank in range(2, number_of + 1)]
    spare, counts = total - limit - (number_of - 1), [1] * (number_of - 1)
    while spare > 0:
        movable = [i for i in range(number_of - 1) if counts[i] < limit]
        pool, remaining = sum([portions[i] for i in movable]), spare
        for i in movable:
            more = min(limit - counts[i], max(1, remaining * portions[i] // pool), spare)
            counts[i] = counts[i] + more
            spare = spare - more
    return np.array([limit] + counts)


def uneven_parts(own_key, count, total, reach, skew):
    if count == 2:
        one = jax.random.randint(own_key, (), max(1, total - reach), min(reach, total - 1) + 1)
        return jnp.stack([one, total - one])
    sizes = jnp.asarray(length_profile(count, total, reach, skew), jnp.int32)
    twos = (count - 1) // 2
    giver, taker = sizes[1:1 + 2 * twos:2], sizes[2:2 + 2 * twos:2]
    margin = jnp.minimum(giver - 1, reach - taker)
    shifted = jax.random.randint(jax.random.fold_in(own_key, 1), (twos,), 0, 1 << 20) % (margin + 1)
    sizes = sizes.at[1:1 + 2 * twos:2].set(giver - shifted).at[2:2 + 2 * twos:2].set(taker + shifted)
    return sizes[jax.random.permutation(jax.random.fold_in(own_key, 2), count)]


def bell_draw(key, shape, scale, reach, cuts=(), held_as=jnp.bfloat16):
    values = jax.random.normal(key, shape, jnp.float32) * scale
    if len(cuts) > 0:
        values = level_of(key, shape, cuts, -0.22, 0.18) * values
    return jnp.clip(values, min=-reach, max=reach).astype(held_as)


def setup_inputs(seed: int = 0) -> dict:
    key_of = jax.random.split(jax.random.key(seed), 9)
    queries = draw_queries(jax.random.fold_in(key_of[8], 71), 0)
    keys = draw_keys(jax.random.fold_in(key_of[8], 71), 0)
    values = bell_draw(key_of[2], (TOKENS, KV * E), 1.0, 6.0, ((0, 64), (1, 8)))
    cotangent = bell_draw(key_of[3], (TOKENS, HQ * E), 1.0, 6.0, ((0, 64), (1, 8)))
    seg_lengths = uneven_parts(key_of[4], SEGS, TOKENS, SEG_MOST, 2).astype(jnp.int32)
    seg_return = jnp.clip(jax.random.uniform(key_of[5], (SEGS,), jnp.float32, -1.0, 1.0), -1.0, 1.0)
    owner_slot = jax.random.permutation(key_of[6], TOKENS).astype(jnp.int32)
    ref_term = jnp.clip(jax.random.uniform(key_of[7], (TOKENS,), jnp.float32, -1.0, 1.0) * level_of(key_of[7], (TOKENS,), ((0, 512),), -0.4, 0.0), -1.0, 1.0)
    return {"queries": queries, "keys": keys, "values": values, "cotangent": cotangent, "seg_lengths": seg_lengths, "seg_return": seg_return, "owner_slot": owner_slot, "ref_term": ref_term}


NEG = -1e+30
HIGH = lax.Precision.HIGHEST

def row_positions():
    row_index = jnp.arange(TOKENS, dtype=jnp.int32)
    half_rows = TOK_DEV // 2
    device = row_index // TOK_DEV
    within = row_index % TOK_DEV
    upper_half = within >= half_rows
    late = (2 * N_CTX - 1 - device) * half_rows + within - half_rows
    early = device * half_rows + within
    return jnp.where(upper_half, late, early).astype(jnp.int32)

def stored_rows():
    position = jnp.arange(TOKENS, dtype=jnp.int32)
    half_rows = TOK_DEV // 2
    block = position // half_rows
    upper_half = block >= N_CTX
    device = jnp.where(upper_half, 2 * N_CTX - 1 - block, block)
    return (device * TOK_DEV + jnp.where(upper_half, half_rows, 0) + position % half_rows).astype(jnp.int32)

def head_grads(head_parts):
    q_head, g_head, k_head, v_head = head_parts
    block_rows = min(512, TOKENS)
    block_count = TOKENS // block_rows
    score_scale = 1.0 / math.sqrt(E)
    key_pos = jnp.arange(TOKENS, dtype=jnp.int32)
    q_blocks = q_head.reshape(GROUP, block_count, block_rows, E).transpose(1, 0, 2, 3)
    g_blocks = g_head.reshape(GROUP, block_count, block_rows, E).transpose(1, 0, 2, 3)
    pos_blocks = key_pos.reshape(block_count, block_rows)

    def step_block(carry, inputs):
        key_accum, value_accum = carry
        q_block, g_block, q_pos = inputs
        allowed = key_pos[None, :] <= q_pos[:, None]
        scores = jnp.einsum('gqe,ke->gqk', q_block, k_head, precision=HIGH) * score_scale
        masked = jnp.where(allowed, scores, NEG)
        row_max = lax.optimization_barrier(jnp.max(masked, axis=-1))
        log_total = row_max + jnp.log(lax.optimization_barrier(jnp.sum(jnp.exp(masked - row_max[..., None]), axis=-1)))
        prob_tile = jnp.where(allowed, jnp.exp(scores - log_total[..., None]), 0.0)
        dot_prod = jnp.einsum('gqe,ke->gqk', g_block, v_head, precision=HIGH)
        row_term = lax.optimization_barrier(jnp.sum(prob_tile * dot_prod, axis=-1))
        slope = (prob_tile * (dot_prod - row_term[..., None])).astype(jnp.bfloat16)
        prob_low = prob_tile.astype(jnp.bfloat16)
        slope_wide = lax.optimization_barrier(slope).astype(jnp.float32)
        prob_wide = lax.optimization_barrier(prob_low).astype(jnp.float32)
        grad_query = jnp.einsum('gqk,ke->gqe', slope_wide, k_head, precision=HIGH) * score_scale
        key_accum = key_accum + jnp.einsum('gqk,gqe->ke', slope_wide, q_block, precision=HIGH) * score_scale
        value_accum = value_accum + jnp.einsum('gqk,gqe->ke', prob_wide, g_block, precision=HIGH)
        return ((key_accum, value_accum), grad_query)
    start_accum = (jnp.zeros((TOKENS, E), jnp.float32), jnp.zeros((TOKENS, E), jnp.float32))
    (key_grad, value_grad), query_grads = lax.scan(step_block, start_accum, (q_blocks, g_blocks, pos_blocks))
    query_grad = query_grads.transpose(1, 0, 2, 3).reshape(GROUP, TOKENS, E)
    return (query_grad, key_grad, value_grad)

def reference(queries, keys, values, cotangent, seg_lengths, seg_return, owner_slot, ref_term):
    order = stored_rows()
    back = row_positions()
    position = jnp.arange(TOKENS, dtype=jnp.int32)
    ends = jnp.cumsum(seg_lengths).astype(jnp.int32)
    starts = (ends - seg_lengths).astype(jnp.int32)
    inside = (position[:, None] >= starts[None, :]) & (position[:, None] < ends[None, :])
    seg_term = lax.optimization_barrier(jnp.sum(jnp.where(inside, seg_return[None, :], 0.0), axis=1))
    weight = jnp.exp(seg_term - ref_term[owner_slot[order]])
    grad_out = (weight[:, None] * cotangent[order].astype(jnp.float32)).astype(jnp.bfloat16)
    grad_wide = lax.optimization_barrier(grad_out).astype(jnp.float32)
    q_heads = queries[order].astype(jnp.float32).reshape(TOKENS, KV, GROUP, E).transpose(1, 2, 0, 3)
    g_heads = grad_wide.reshape(TOKENS, KV, GROUP, E).transpose(1, 2, 0, 3)
    k_heads = keys[order].astype(jnp.float32).reshape(TOKENS, KV, E).transpose(1, 0, 2)
    v_heads = values[order].astype(jnp.float32).reshape(TOKENS, KV, E).transpose(1, 0, 2)
    query_grad, key_grad, value_grad = lax.map(head_grads, (q_heads, g_heads, k_heads, v_heads))
    grad_queries = query_grad.transpose(2, 0, 1, 3).reshape(TOKENS, KV * GROUP * E)[back].astype(jnp.bfloat16)
    grad_keys = key_grad.transpose(1, 0, 2).reshape(TOKENS, KV * E)[back].astype(jnp.bfloat16)
    grad_values = value_grad.transpose(1, 0, 2).reshape(TOKENS, KV * E)[back].astype(jnp.bfloat16)
    return (grad_queries, grad_keys, grad_values)
```

```python
import functools
import math

import jax
import jax.numpy as jnp
from jax import lax
from jax.experimental import pallas as pl
from jax.experimental.pallas import tpu as pltpu
from jax.sharding import Mesh, PartitionSpec as P

E = 128
GROUP = 6
HALF = 64
ROWS = 2 * HALF
TEAM = 4
QUADS = 4
RING = 4
TILE = RING * HALF
HEAD_COLS = TEAM * HALF
COLS = GROUP * HEAD_COLS
LAST = 2 * (2 * QUADS * RING) * 2 - 1
NEG = -1e30
SCALE = 1.0 / math.sqrt(E)
SCALE2 = SCALE * math.log2(math.e)
LOG2E = math.log2(math.e)
F32 = jnp.float32
BF16 = jnp.bfloat16
I32 = jnp.int32
VMEM = 48 * 1024 * 1024


def dot(left, right, left_dim, right_dim):
    return lax.dot_general(
        left, right, (((left_dim,), (right_dim,)), ((), ())), preferred_element_type=F32
    )


def iota(shape, dim):
    return lax.broadcasted_iota(I32, shape, dim)


def call(kernel, outs, scratch=(), scalars=0, inputs=0, cost=None):
    spec = pl.BlockSpec(memory_space=pltpu.VMEM)
    return pl.pallas_call(
        kernel,
        out_shape=outs,
        in_specs=[pl.BlockSpec(memory_space=pltpu.SMEM)] * scalars + [spec] * inputs,
        out_specs=jax.tree.map(lambda _: spec, outs),
        scratch_shapes=list(scratch),
        compiler_params=pltpu.CompilerParams(vmem_limit_bytes=VMEM),
        cost_estimate=cost,
    )


def pack_kernel(q_ref, g_ref, slot_ref, k_ref, v_ref, qg_ref, kv_ref):
    width = GROUP * E
    qg_ref[:ROWS, :width] = q_ref[...]
    qg_ref[:ROWS, width:] = g_ref[...]
    slot = slot_ref[...]
    row = iota((16, ROWS), 0)
    coded = jnp.where(row == 0, slot >> 7, jnp.where(row == 1, slot & 127, 0))
    qg_ref[ROWS:, :] = jnp.zeros((16, 2 * width), BF16)
    qg_ref[ROWS:, :ROWS] = coded.astype(F32).astype(BF16)
    for copy in range(QUADS):
        kv_ref[copy, :, :E] = k_ref[...]
        kv_ref[copy, :, E:] = v_ref[...]


def arrange(slots, refs, first, out_ref):
    for group in range(2):
        for head in range(GROUP):
            for ref, slot in zip(refs, slots):
                start = pl.multiple_of(head * HEAD_COLS + slot * HALF, HALF)
                column = first + head * E
                out_ref[group, pl.ds(start, HALF), :] = ref[
                    group * HALF : (group + 1) * HALF, column : column + E
                ]


def place(where_ref):
    quad, pair, ring, core = (where_ref[i] for i in range(4))
    mine = 2 * pair + core
    return quad, pair, ring, core, (mine, mine ^ 1, mine ^ 2, mine ^ 3)


def causal_mask(group, quad, pair, ring, core):
    key_row = iota((TILE, 1), 0)
    key_owner = 2 * ((2 * quad + pair) * RING + (key_row >> 6)) + core
    column = iota((1, HEAD_COLS), 1)
    slot = column >> 6
    query_owner = 2 * ((2 * quad + (slot >> 1)) * RING + ring) + (slot & 1)
    if group == 1:
        key_owner, query_owner = LAST - key_owner, LAST - query_owner
    key_pos = key_owner * HALF + (key_row & 63)
    query_pos = query_owner * HALF + (column & 63)
    return key_pos <= query_pos


def free_visit(index, quad):
    wide = index < QUADS
    rest = index - QUADS
    early = rest < quad
    group = jnp.where(wide, 1, jnp.where(early, 0, 1))
    half = jnp.where(wide, 0, jnp.where(early, 0, 1))
    part = jnp.where(wide, index, jnp.where(early, rest, rest + 1))
    return group, half, part


def key_value_tile(kv_ref, half, part):
    start = pl.multiple_of(half * HALF, HALF)
    return kv_ref[:, part, pl.ds(start, HALF), :].reshape(TILE, 2 * E)


def forward_kernel(
    where_ref, qg0_ref, qg1_ref, qg2_ref, qg3_ref, kv_ref, table_ref, length_ref, return_ref,
    stat_ref, qs_ref, gs_ref, top_ref, sum_ref, term_ref,
):
    quad, pair, ring, core, slots = place(where_ref)
    refs = (qg0_ref, qg1_ref, qg2_ref, qg3_ref)
    arrange(slots, refs, 0, qs_ref)
    arrange(slots, refs, GROUP * E, gs_ref)
    top_ref[...] = jnp.full(top_ref.shape, NEG, F32)
    sum_ref[...] = jnp.zeros(sum_ref.shape, F32)
    term_ref[...] = jnp.zeros(term_ref.shape, F32)

    def visit(group, half, part, mask):
        key_value = key_value_tile(kv_ref, half, part)
        key, value = key_value[:, :E], key_value[:, E:]
        for head in range(GROUP):
            cols = slice(head * HEAD_COLS, (head + 1) * HEAD_COLS)
            scores = dot(key, qs_ref[group, cols, :], 1, 1) * SCALE2
            dots = dot(value, gs_ref[group, cols, :], 1, 1)
            if mask is not None:
                scores = jnp.where(mask, scores, NEG)
            scores = scores.reshape(TILE // 8, 8, HEAD_COLS)
            dots = dots.reshape(TILE // 8, 8, HEAD_COLS)
            old = top_ref[group, :, cols]
            top = jnp.maximum(old, jnp.max(scores, axis=0))
            factor = jnp.exp2(old - top)
            prob = jnp.exp2(scores - top[None])
            top_ref[group, :, cols] = top
            sum_ref[group, :, cols] = factor * sum_ref[group, :, cols] + jnp.sum(prob, axis=0)
            term_ref[group, :, cols] = factor * term_ref[group, :, cols] + jnp.sum(
                prob * dots, axis=0
            )

    @pl.loop(0, 2 * QUADS - 1)
    def _(index):
        visit(*free_visit(index, quad), None)

    for group in range(2):
        visit(group, group, quad, causal_mask(group, quad, pair, ring, core))

    stat_ref[...] = jnp.zeros(stat_ref.shape, F32)
    for group in range(2):
        top = top_ref[group]
        best = jnp.max(top, axis=0, keepdims=True)
        factor = jnp.exp2(top - best)
        stat_ref[3 * group : 3 * group + 1, :] = best
        stat_ref[3 * group + 1 : 3 * group + 2, :] = jnp.sum(
            factor * sum_ref[group], axis=0, keepdims=True
        )
        stat_ref[3 * group + 2 : 3 * group + 3, :] = jnp.sum(
            factor * term_ref[group], axis=0, keepdims=True
        )

    table = table_ref[...].reshape(QUADS * RING * 8, E)
    high = table.astype(BF16)
    rest = table - high.astype(F32)
    middle = rest.astype(BF16)
    low = (rest - middle.astype(F32)).astype(BF16)
    lane = iota((E, ROWS), 0)
    line = iota((8, ROWS), 0)
    block = jnp.zeros((8, ROWS), F32)
    for ref, slot in zip(refs, slots):
        code = ref[ROWS : ROWS + 16, :ROWS].astype(F32)
        owner = code[0:1].astype(I32)
        entry = code[1:2].astype(I32)
        pick = (lane == (entry & 15)).astype(F32).astype(BF16)
        picked = dot(high, pick, 1, 0) + dot(middle, pick, 1, 0) + dot(low, pick, 1, 0)
        row = ((owner >> 4) * RING + ((owner >> 1) & 3)) * 8 + (entry >> 4)
        held = (((owner >> 3) & 1) == pair) & ((owner & 1) == core)
        row = jnp.where(held, row, -1)
        part = jnp.sum(jnp.where(lane == row, picked, 0.0), axis=0, keepdims=True)
        block = jnp.where(line == slot, part, block)
    before = iota((E, E), 1) <= iota((E, E), 0)
    ends = jnp.sum(
        jnp.where(before, length_ref[...].astype(F32), 0.0), axis=1, keepdims=True
    )
    own = iota((E, E), 1) == iota((E, E), 0)
    lengths = jnp.sum(jnp.where(own, length_ref[...].astype(F32), 0.0), axis=1, keepdims=True)
    returns = jnp.sum(jnp.where(own, return_ref[...], 0.0), axis=1, keepdims=True)
    starts = ends - lengths
    column = iota((1, ROWS), 1)
    for slot in range(TEAM):
        owner = 2 * ((2 * quad + slot // 2) * RING + ring) + slot % 2
        place_of = jnp.where(column < HALF, owner, LAST - owner)
        pos = (place_of * HALF + (column & 63)).astype(F32)
        inside = (pos >= starts) & (pos < ends)
        part = jnp.sum(jnp.where(inside, returns, 0.0), axis=0, keepdims=True)
        block = jnp.where(line == TEAM + slot, part, block)
    stat_ref[8:16, :ROWS] = block


def backward_kernel(
    where_ref, qg0_ref, qg1_ref, qg2_ref, qg3_ref, kv_ref,
    stat0_ref, stat1_ref, stat2_ref, stat3_ref,
    dkv_ref, dq0_ref, dqc_ref, dq2_ref,
    qs_ref, gs_ref, dqt_ref, acc_ref, shift_ref, term_ref, prob_ref, slope_ref, turn_ref,
):
    quad, pair, ring, core, slots = place(where_ref)
    refs = (qg0_ref, qg1_ref, qg2_ref, qg3_ref)
    stats = (stat0_ref, stat1_ref, stat2_ref, stat3_ref)
    arrange(slots, refs, 0, qs_ref)
    arrange(slots, refs, GROUP * E, gs_ref)
    dqt_ref[...] = jnp.zeros(dqt_ref.shape, F32)
    acc_ref[...] = jnp.zeros(acc_ref.shape, F32)
    logw = [
        stat0_ref[12 + s : 13 + s, :ROWS] - sum(st[8 + s : 9 + s, :ROWS] for st in stats)
        for s in range(TEAM)
    ]
    low_lane = iota((1, ROWS), 1) < HALF
    for group in range(2):
        tops = [st[3 * group : 3 * group + 1, :] for st in stats]
        best = functools.reduce(jnp.maximum, tops)
        factors = [jnp.exp2(top - best) for top in tops]
        total = sum(f * st[3 * group + 1 : 3 * group + 2, :] for f, st in zip(factors, stats))
        term = sum(f * st[3 * group + 2 : 3 * group + 3, :] for f, st in zip(factors, stats))
        shift = best + jnp.log2(total)
        term_ref[group] = term / total
        pieces = []
        for first in (0, 2):
            a, b = logw[first], logw[first + 1]
            if group == 0:
                b = pltpu.roll(jnp.broadcast_to(b, (8, ROWS)), HALF, 1)[0:1]
            else:
                a = pltpu.roll(jnp.broadcast_to(a, (8, ROWS)), HALF, 1)[0:1]
            pieces.append(jnp.where(low_lane, a, b))
        weights = jnp.concatenate(pieces, axis=1) * LOG2E
        for head in range(GROUP):
            cols = slice(head * HEAD_COLS, (head + 1) * HEAD_COLS)
            shift_ref[group, :, cols] = shift[:, cols] - weights

    def visit(group, half, part, mask):
        key_value = key_value_tile(kv_ref, half, part)
        key, value = key_value[:, :E], key_value[:, E:]
        for head in range(GROUP):
            cols = slice(head * HEAD_COLS, (head + 1) * HEAD_COLS)
            scores = dot(key, qs_ref[group, cols, :], 1, 1) * SCALE2
            dots = dot(value, gs_ref[group, cols, :], 1, 1)
            if mask is not None:
                scores = jnp.where(mask, scores, NEG)
            prob = jnp.exp2(scores - shift_ref[group, :, cols])
            prob_ref[:, cols] = prob.astype(BF16)
            slope_ref[:, cols] = (prob * (dots - term_ref[group, :, cols])).astype(BF16)
        slope = slope_ref[...]
        acc_ref[half, part, :, :E] += dot(slope, qs_ref[group], 1, 0)
        acc_ref[half, part, :, E:] += dot(prob_ref[...], gs_ref[group], 1, 0)
        dqt_ref[group] += dot(key, slope, 0, 0)

    @pl.loop(0, 2 * QUADS - 1)
    def _(index):
        visit(*free_visit(index, quad), None)

    for group in range(2):
        visit(group, group, quad, causal_mask(group, quad, pair, ring, core))

    scales = jnp.where(iota((1, 2 * E), 1) < E, SCALE, 1.0)
    for half in range(2):
        for part in range(QUADS):
            tile = (acc_ref[half, part] * scales).astype(BF16)
            dkv_ref[:, part, half * HALF : (half + 1) * HALF, :] = tile.reshape(RING, HALF, 2 * E)
    targets = (dq0_ref, dqc_ref.at[0], dq2_ref, dqc_ref.at[1])
    for group in range(2):
        for head in range(GROUP):
            cols = slice(head * HEAD_COLS, (head + 1) * HEAD_COLS)
            turn_ref[...] = dqt_ref[group, :, cols].T * SCALE
            for ref, slot in zip(targets, slots):
                start = pl.multiple_of(slot * HALF, HALF)
                ref[group * HALF : (group + 1) * HALF, head * E : (head + 1) * E] = turn_ref[
                    pl.ds(start, HALF), :
                ].astype(ref.dtype)


def shape(dims, dtype):
    return jax.ShapeDtypeStruct(dims, dtype)


def swapped(x, axis):
    return lax.ppermute(x, axis, [(0, 1), (1, 0)])


def both_swapped(x):
    return lax.ppermute(x, ("pair", "core"), [(i, 3 - i) for i in range(4)])


def per_device(queries, keys, values, cotangent, seg_lengths, seg_return, owner_slot, ref_term):
    quad, pair = lax.axis_index("quad"), lax.axis_index("pair")
    ring, core = lax.axis_index("ring"), lax.axis_index("core")
    where = jnp.stack([quad, pair, ring, core]).astype(I32)
    width = GROUP * E

    qg, kv_own = call(
        pack_kernel,
        (shape((ROWS + 16, 2 * width), BF16), shape((QUADS, ROWS, 2 * E), BF16)),
        inputs=5,
    )(queries, cotangent, owner_slot.reshape(1, ROWS), keys, values)

    head = lax.axis_index("col") * 2 + lax.axis_index("far")
    terms = jnp.pad(ref_term.reshape(1, 16), ((0, 7), (0, E - 16)))
    terms = jnp.where(iota((8, E), 0) == head, terms[0:1], 0.0)
    terms = terms + swapped(terms, "far")
    for step in (1, 2):
        terms = terms + lax.ppermute(terms, "col", [(i, i ^ step) for i in range(4)])

    kv_z = lax.all_to_all(kv_own, "quad", 0, 0, tiled=True)
    qg1 = swapped(qg, "core")
    qg2 = swapped(qg, "pair")
    qg3 = swapped(qg2, "core")
    kv_all = lax.all_to_all(
        jnp.broadcast_to(kv_z[None], (RING, QUADS, ROWS, 2 * E)), "ring", 0, 0, tiled=True
    )
    table = lax.all_to_all(
        jnp.broadcast_to(terms[None], (QUADS * RING, 8, E)), ("quad", "ring"), 0, 0, tiled=True
    )
    team = (qg, qg1, qg2, qg3)
    pairs = 9 * TILE * COLS
    kv_scratch = [pltpu.VMEM((2, COLS, E), BF16), pltpu.VMEM((2, COLS, E), BF16)]
    stat = call(
        forward_kernel,
        shape((16, COLS), F32),
        kv_scratch + [pltpu.VMEM((2, 8, COLS), F32)] * 3,
        scalars=1,
        inputs=8,
        cost=pl.CostEstimate(flops=4 * E * pairs, bytes_accessed=4 << 20, transcendentals=pairs),
    )(where, *team, kv_all, table, seg_lengths.reshape(1, E), seg_return.reshape(1, E))

    stats = (stat, swapped(stat, "core"), swapped(stat, "pair"), both_swapped(stat))
    dkv, dq0, dqc, dq2 = call(
        backward_kernel,
        (
            shape((RING, QUADS, ROWS, 2 * E), BF16),
            shape((ROWS, width), F32),
            shape((2, ROWS, width), BF16),
            shape((ROWS, width), F32),
        ),
        kv_scratch
        + [
            pltpu.VMEM((2, E, COLS), F32),
            pltpu.VMEM((2, QUADS, TILE, 2 * E), F32),
            pltpu.VMEM((2, 1, COLS), F32),
            pltpu.VMEM((2, 1, COLS), F32),
            pltpu.VMEM((TILE, COLS), BF16),
            pltpu.VMEM((TILE, COLS), BF16),
            pltpu.VMEM((HEAD_COLS, E), F32),
        ],
        scalars=1,
        inputs=9,
        cost=pl.CostEstimate(flops=10 * E * pairs, bytes_accessed=5 << 20, transcendentals=pairs),
    )(where, *team, kv_all, *stats)

    from_core = swapped(dqc, "core").astype(F32)
    from_pair = swapped((dq2 + from_core[1]).astype(BF16), "pair").astype(F32)
    grad_queries = (dq0 + from_core[0] + from_pair).astype(BF16)

    parts = lax.all_to_all(dkv, "ring", 0, 0, tiled=True)
    parts = jnp.sum(parts.astype(F32), axis=0).astype(BF16)
    parts = lax.all_to_all(parts, "quad", 0, 0, tiled=True)
    kv_grad = jnp.sum(parts.astype(F32), axis=0).astype(BF16)
    return grad_queries, kv_grad[:, :E], kv_grad[:, E:]


def solution(mesh):
    fine = Mesh(
        mesh.devices.reshape(QUADS, 2, RING, 2, 4, 2),
        ("quad", "pair", "ring", "core", "col", "far"),
    )
    ctx = ("quad", "pair", "ring", "core")
    head = ("col", "far")
    return jax.shard_map(
        per_device,
        mesh=fine,
        in_specs=(
            P(ctx, head), P(ctx, head), P(ctx, head), P(ctx, head),
            P(), P(), P(ctx), P(ctx + head),
        ),
        out_specs=(P(ctx, head), P(ctx, head), P(ctx, head)),
        check_vma=False,
    )
```

```python
import functools
import math

import jax
import jax.numpy as jnp
from jax import lax
from jax.experimental import pallas as pl
from jax.experimental.pallas import tpu as pltpu
from jax.sharding import Mesh, PartitionSpec as P

E = 128
GROUP = 6
HALF = 64
ROWS = 2 * HALF
TEAM = 4
LINE = 8
PARTS = LINE // 2
TILE = 4 * HALF
HEAD_COLS = TEAM * HALF
COLS = GROUP * HEAD_COLS
LAST = 2 * (LINE * TEAM * 2) - 1
NEG = -1e30
SCALE = 1.0 / math.sqrt(E)
SCALE2 = SCALE * math.log2(math.e)
LOG2E = math.log2(math.e)
F32 = jnp.float32
BF16 = jnp.bfloat16
I32 = jnp.int32
VMEM = 24 * 1024 * 1024


def dot(left, right, left_dim, right_dim):
    return lax.dot_general(
        left, right, (((left_dim,), (right_dim,)), ((), ())), preferred_element_type=F32
    )


def iota(shape, dim):
    return lax.broadcasted_iota(I32, shape, dim)


def call(kernel, outs, scratch=(), scalars=0, inputs=0, cost=None):
    spec = pl.BlockSpec(memory_space=pltpu.VMEM)
    return pl.pallas_call(
        kernel,
        out_shape=outs,
        in_specs=[pl.BlockSpec(memory_space=pltpu.SMEM)] * scalars + [spec] * inputs,
        out_specs=jax.tree.map(lambda _: spec, outs),
        scratch_shapes=list(scratch),
        compiler_params=pltpu.CompilerParams(vmem_limit_bytes=VMEM),
        cost_estimate=cost,
    )


def pack_kernel(
    where_ref, q_ref, g_ref, slot_ref, length_ref, return_ref, qg_ref, seg_ref
):
    line_place, core = where_ref[0], where_ref[2]
    width = GROUP * E
    qg_ref[0, :ROWS, :] = q_ref[...]
    qg_ref[1, :ROWS, :] = g_ref[...]
    slot = slot_ref[...]
    row = iota((16, ROWS), 0)
    coded = jnp.where(row == 0, slot >> 7, jnp.where(row == 1, slot & 127, 0))
    qg_ref[:, ROWS:, :] = jnp.zeros((2, 16, width), BF16)
    qg_ref[0, ROWS:, :ROWS] = coded.astype(F32).astype(BF16)

    lengths_row = length_ref[...].astype(F32)
    before = iota((E, E), 1) <= iota((E, E), 0)
    own = iota((E, E), 1) == iota((E, E), 0)
    ends = jnp.sum(jnp.where(before, lengths_row, 0.0), axis=1, keepdims=True)
    lengths = jnp.sum(jnp.where(own, lengths_row, 0.0), axis=1, keepdims=True)
    returns = jnp.sum(jnp.where(own, return_ref[...], 0.0), axis=1, keepdims=True)
    starts = ends - lengths
    column = iota((1, ROWS), 1)
    line = iota((8, ROWS), 0)
    block = jnp.zeros((8, ROWS), F32)
    for slot in range(TEAM):
        owner = 2 * (line_place * TEAM + slot) + core
        place_of = jnp.where(column < HALF, owner, LAST - owner)
        pos = (place_of * HALF + (column & 63)).astype(F32)
        inside = (pos >= starts) & (pos < ends)
        part = jnp.sum(jnp.where(inside, returns, 0.0), axis=0, keepdims=True)
        block = jnp.where(line == TEAM + slot, part, block)
    seg_ref[...] = block


def arrange(slots, refs, out_ref):
    for group in range(2):
        for head in range(GROUP):
            for ref, slot in zip(refs, slots):
                start = pl.multiple_of(head * HEAD_COLS + slot * HALF, HALF)
                out_ref[group, pl.ds(start, HALF), :] = ref[
                    group * HALF : (group + 1) * HALF, head * E : (head + 1) * E
                ]


def place(where_ref):
    z, ring, core = (where_ref[i] for i in range(3))
    return z, ring, core, [(ring - step) & 3 for step in range(TEAM)]


def causal_mask(group, z, ring, core):
    key_row = iota((TILE, 1), 0)
    piece = key_row >> 6
    key_owner = 2 * (((z & 6) + (piece & 1)) * TEAM + ring) + (core ^ (piece >> 1))
    column = iota((1, HEAD_COLS), 1)
    query_owner = 2 * (z * TEAM + (column >> 6)) + core
    if group == 1:
        key_owner, query_owner = LAST - key_owner, LAST - query_owner
    key_pos = key_owner * HALF + (key_row & 63)
    query_pos = query_owner * HALF + (column & 63)
    return key_pos <= query_pos


def free_visit(index, edge):
    wide = index < PARTS
    rest = index - PARTS
    early = rest < edge
    group = jnp.where(wide, 1, jnp.where(early, 0, 1))
    half = jnp.where(wide, 0, jnp.where(early, 0, 1))
    part = jnp.where(wide, index, jnp.where(early, rest, rest + 1))
    return group, half, part


def key_value_tile(kv_refs, half, part):
    rows = pl.ds(pl.multiple_of(half * HALF, HALF), HALF)
    pieces = [ref[pl.ds(part * 2, 2), rows, :].reshape(2 * HALF, 2 * E) for ref in kv_refs]
    return jnp.concatenate(pieces, axis=0)


def forward_kernel(
    where_ref, qg0_ref, qg1_ref, q2_ref, g2_ref, qg3_ref, kv0_ref, kv1_ref,
    stat_ref, qs_ref, gs_ref, top_ref, sum_ref, term_ref,
):
    z, ring, core, slots = place(where_ref)
    arrange(slots, (qg0_ref.at[0], qg1_ref.at[0], q2_ref, qg3_ref.at[0]), qs_ref)
    arrange(slots, (qg0_ref.at[1], qg1_ref.at[1], g2_ref, qg3_ref.at[1]), gs_ref)
    kv_refs = (kv0_ref, kv1_ref)
    edge = z >> 1
    top_ref[...] = jnp.full(top_ref.shape, NEG, F32)
    sum_ref[...] = jnp.zeros(sum_ref.shape, F32)
    term_ref[...] = jnp.zeros(term_ref.shape, F32)

    def visit(group, half, part, mask):
        key_value = key_value_tile(kv_refs, half, part)
        key, value = key_value[:, :E], key_value[:, E:]
        for head in range(GROUP):
            cols = slice(head * HEAD_COLS, (head + 1) * HEAD_COLS)
            scores = dot(key, qs_ref[group, cols, :], 1, 1) * SCALE2
            dots = dot(value, gs_ref[group, cols, :], 1, 1)
            if mask is not None:
                scores = jnp.where(mask, scores, NEG)
            scores = scores.reshape(TILE // 8, 8, HEAD_COLS)
            dots = dots.reshape(TILE // 8, 8, HEAD_COLS)
            old = top_ref[group, :, cols]
            top = jnp.maximum(old, jnp.max(scores, axis=0))
            factor = jnp.exp2(old - top)
            prob = jnp.exp2(scores - top[None])
            top_ref[group, :, cols] = top
            sum_ref[group, :, cols] = factor * sum_ref[group, :, cols] + jnp.sum(prob, axis=0)
            term_ref[group, :, cols] = factor * term_ref[group, :, cols] + jnp.sum(
                prob * dots, axis=0
            )

    @pl.loop(0, 2 * PARTS - 1)
    def _(index):
        visit(*free_visit(index, edge), None)

    for group in range(2):
        visit(group, group, edge, causal_mask(group, z, ring, core))

    stat_ref[...] = jnp.zeros(stat_ref.shape, F32)
    for group in range(2):
        top = top_ref[group]
        best = jnp.max(top, axis=0, keepdims=True)
        factor = jnp.exp2(top - best)
        stat_ref[3 * group : 3 * group + 1, :] = best
        stat_ref[3 * group + 1 : 3 * group + 2, :] = jnp.sum(
            factor * sum_ref[group], axis=0, keepdims=True
        )
        stat_ref[3 * group + 2 : 3 * group + 3, :] = jnp.sum(
            factor * term_ref[group], axis=0, keepdims=True
        )


def lookup_kernel(
    where_ref, qg0_ref, qg1_ref, q2_ref, g2_ref, qg3_ref, stat_ref, table_ref, seg_ref, out_ref
):
    z, ring, core, slots = place(where_ref)
    refs = (qg0_ref.at[0], qg1_ref.at[0], q2_ref, qg3_ref.at[0])
    table = table_ref[:, 0, :]
    high = table.astype(BF16)
    rest = table - high.astype(F32)
    middle = rest.astype(BF16)
    low = (rest - middle.astype(F32)).astype(BF16)
    lane = iota((E, ROWS), 0)
    device = iota((2 * LINE, ROWS), 0)
    line = iota((8, ROWS), 0)
    block = seg_ref[...]
    for ref, slot in zip(refs, slots):
        code = ref[ROWS : ROWS + 16, :ROWS].astype(F32)
        owner = code[0:1].astype(I32)
        entry = code[1:2].astype(I32)
        pick = (lane == entry).astype(F32).astype(BF16)
        picked = dot(high, pick, 1, 0) + dot(middle, pick, 1, 0) + dot(low, pick, 1, 0)
        line_place = (owner >> 3) ^ jnp.where(((entry >> 4) & 1) == where_ref[3], 0, 4)
        row = jnp.where(((owner >> 1) & 3) == ring, line_place * 2 + (owner & 1), -1)
        part = jnp.sum(jnp.where(device == row, picked, 0.0), axis=0, keepdims=True)
        block = jnp.where(line == slot, part, block)
    for copy in range(TEAM):
        out_ref[copy] = stat_ref[...]
        for row in range(8):
            out_ref[copy, 6:7, row * ROWS : (row + 1) * ROWS] = block[row : row + 1]


def row_weights(stats):
    logw = [
        stats[0][6:7, (TEAM + s) * ROWS : (TEAM + s + 1) * ROWS]
        - sum(st[6:7, s * ROWS : (s + 1) * ROWS] for st in stats)
        for s in range(TEAM)
    ]
    low_lane = iota((1, ROWS), 1) < HALF
    groups = []
    for group in range(2):
        pieces = []
        for first in (0, 2):
            a, b = logw[first], logw[first + 1]
            if group == 0:
                b = pltpu.roll(jnp.broadcast_to(b, (8, ROWS)), HALF, 1)[0:1]
            else:
                a = pltpu.roll(jnp.broadcast_to(a, (8, ROWS)), HALF, 1)[0:1]
            pieces.append(jnp.where(low_lane, a, b))
        groups.append(jnp.concatenate(pieces, axis=1))
    return groups


def merge_stats(stat_ref, shift_ref, term_ref):
    stats = [stat_ref.at[s] for s in range(TEAM)]
    weights = row_weights(stats)
    for group in range(2):
        tops = [st[3 * group : 3 * group + 1, :] for st in stats]
        best = functools.reduce(jnp.maximum, tops)
        factors = [jnp.exp2(top - best) for top in tops]
        total = sum(f * st[3 * group + 1 : 3 * group + 2, :] for f, st in zip(factors, stats))
        term = sum(f * st[3 * group + 2 : 3 * group + 3, :] for f, st in zip(factors, stats))
        shift = best + jnp.log2(total)
        term_ref[group] = term / total
        for head in range(GROUP):
            cols = slice(head * HEAD_COLS, (head + 1) * HEAD_COLS)
            shift_ref[group, :, cols] = shift[:, cols] - weights[group] * LOG2E


def backward_kernel(
    where_ref, qg0_ref, qg1_ref, q2_ref, g2_ref, qg3_ref, kv0_ref, kv1_ref, stat_ref,
    dkv0_ref, dkv1_ref, dq0_ref, dq1_ref, dq2_ref, dq3_ref,
    qs_ref, gs_ref, dqt_ref, acc_ref, shift_ref, term_ref, prob_ref, slope_ref, turn_ref,
):
    z, ring, core, slots = place(where_ref)
    kv_refs = (kv0_ref, kv1_ref)
    arrange(slots, (qg0_ref.at[0], qg1_ref.at[0], q2_ref, qg3_ref.at[0]), qs_ref)
    arrange(slots, (qg0_ref.at[1], qg1_ref.at[1], g2_ref, qg3_ref.at[1]), gs_ref)
    merge_stats(stat_ref, shift_ref, term_ref)
    acc_ref[...] = jnp.zeros(acc_ref.shape, F32)
    dqt_ref[...] = jnp.zeros(dqt_ref.shape, F32)
    edge, pair = z >> 1, z & 1

    def visit(group, half, part, mask):
        key_value = key_value_tile(kv_refs, half, part)
        key, value = key_value[:, :E], key_value[:, E:]
        for head in range(GROUP):
            cols = slice(head * HEAD_COLS, (head + 1) * HEAD_COLS)
            scores = dot(key, qs_ref[group, cols, :], 1, 1) * SCALE2
            dots = dot(value, gs_ref[group, cols, :], 1, 1)
            if mask is not None:
                scores = jnp.where(mask, scores, NEG)
            prob = jnp.exp2(scores - shift_ref[group, :, cols])
            prob_ref[:, cols] = prob.astype(BF16)
            slope_ref[:, cols] = (prob * (dots - term_ref[group, :, cols])).astype(BF16)
        slope = slope_ref[...]
        acc_ref[half, part, :, :E] += dot(slope, qs_ref[group], 1, 0)
        acc_ref[half, part, :, E:] += dot(prob_ref[...], gs_ref[group], 1, 0)
        dqt_ref[group] += dot(key, slope, 0, 0)

    @pl.loop(0, 2 * PARTS - 1)
    def _(index):
        visit(*free_visit(index, edge), None)

    for group in range(2):
        visit(group, group, edge, causal_mask(group, z, ring, core))

    scales = jnp.where(iota((1, 2 * E), 1) < E, SCALE, 1.0)
    for half in range(2):
        for part in range(PARTS):
            tile = (acc_ref[half, part] * scales).reshape(2, 2, HALF, 2 * E)
            rows = slice(half * HALF, (half + 1) * HALF)
            for piece in range(2):
                dkv0_ref[piece ^ pair, part, rows, :] = tile[0, piece]
                dkv1_ref[piece ^ pair, part, rows, :] = tile[1, piece].astype(BF16)
    targets = (dq0_ref, dq1_ref, dq2_ref, dq3_ref)
    for group in range(2):
        for head in range(GROUP):
            cols = slice(head * HEAD_COLS, (head + 1) * HEAD_COLS)
            turn_ref[...] = dqt_ref[group, :, cols].T * SCALE
            for ref, slot in zip(targets, slots):
                start = pl.multiple_of(slot * HALF, HALF)
                ref[group * HALF : (group + 1) * HALF, head * E : (head + 1) * E] = turn_ref[
                    pl.ds(start, HALF), :
                ].astype(ref.dtype)


def shape(dims, dtype):
    return jax.ShapeDtypeStruct(dims, dtype)


def swapped(x, axis):
    return lax.ppermute(x, axis, [(0, 1), (1, 0)])


def far_swapped(x):
    pairs = [(i, i ^ 5) for i in range(LINE)]
    return lax.ppermute(x, ("quad", "far"), pairs)


def from_ring(x, step):
    return lax.ppermute(x, "ring", [(i, (i + step) % TEAM) for i in range(TEAM)])


def per_device(queries, keys, values, cotangent, seg_lengths, seg_return, owner_slot, ref_term):
    head = lax.axis_index(("far_col", "near_col", "far"))
    place_names = (("quad", "pair"), "ring", "core", "far")
    where = jnp.stack([lax.axis_index(name) for name in place_names]).astype(I32)
    width = GROUP * E

    kv_own = jnp.broadcast_to(
        jnp.concatenate([keys, values], axis=1)[None], (LINE, ROWS, 2 * E)
    )
    qg, seg = call(
        pack_kernel,
        (shape((2, ROWS + 16, width), BF16), shape((8, E), F32)),
        scalars=1,
        inputs=5,
    )(
        where, queries, cotangent, owner_slot.reshape(1, ROWS),
        seg_lengths.reshape(1, E), seg_return.reshape(1, E),
    )
    lane = iota((8, E), 1)
    terms = jnp.where((lane >> 4) == head, jnp.tile(ref_term, 8)[None], 0.0)
    terms = terms + far_swapped(terms)
    kv_own, terms, qg = lax.optimization_barrier((kv_own, terms, qg))
    kv0 = lax.all_to_all(kv_own, ("quad", "pair"), 0, 0, tiled=True)
    qg1, qg3 = from_ring(qg, 1), from_ring(qg, 3)
    terms = terms + swapped(terms, "near_col")
    qg1, qg3, terms = lax.optimization_barrier((qg1, qg3, terms))
    terms = terms + swapped(terms, "far_col")
    team = [qg, qg1, from_ring(qg1[0], 1), from_ring(qg3[1], 3), qg3]
    kv0, terms, *team = lax.optimization_barrier((kv0, terms, *team))
    kv1 = swapped(kv0, "core")
    table = lax.all_to_all(
        jnp.broadcast_to(terms[None], (2 * LINE, 8, E)), ("quad", "pair", "core"), 0, 0, tiled=True
    )
    pairs = 9 * TILE * COLS
    kv_scratch = [pltpu.VMEM((2, COLS, E), BF16), pltpu.VMEM((2, COLS, E), BF16)]
    stat = call(
        forward_kernel,
        shape((8, COLS), F32),
        kv_scratch + [pltpu.VMEM((2, 8, COLS), F32)] * 3,
        scalars=1,
        inputs=7,
        cost=pl.CostEstimate(flops=4 * E * pairs, bytes_accessed=4 << 20, transcendentals=pairs),
    )(where, *team, kv0, kv1)
    stat = call(lookup_kernel, shape((TEAM, 8, COLS), F32), scalars=1, inputs=8)(
        where, *team, stat, table, seg
    )
    stats = lax.all_to_all(stat, "ring", 0, 0, tiled=True)
    core_grad = (2, LINE // 2, ROWS, 2 * E)
    query_grad = shape((ROWS, width), BF16)
    grad0, grad1, dq0, *dqs = call(
        backward_kernel,
        (
            shape(core_grad, F32), shape(core_grad, BF16), shape((ROWS, width), F32),
            query_grad, query_grad, query_grad,
        ),
        kv_scratch
        + [
            pltpu.VMEM((2, E, COLS), F32),
            pltpu.VMEM((2, PARTS, TILE, 2 * E), F32),
            pltpu.VMEM((2, 1, COLS), F32),
            pltpu.VMEM((2, 1, COLS), F32),
            pltpu.VMEM((TILE, COLS), BF16),
            pltpu.VMEM((TILE, COLS), BF16),
            pltpu.VMEM((HEAD_COLS, E), F32),
        ],
        scalars=1,
        inputs=8,
        cost=pl.CostEstimate(flops=10 * E * pairs, bytes_accessed=5 << 20, transcendentals=pairs),
    )(where, *team, kv0, kv1, stats)

    own = grad0 + swapped(grad1, "core").astype(F32)
    parts = (own[0] + swapped(own[1].astype(BF16), "pair").astype(F32)).astype(BF16)
    parts = lax.all_to_all(parts, "quad", 0, 0, tiled=True)
    kv_grad = jnp.sum(parts.astype(F32), axis=0).astype(BF16)

    for step, part in enumerate(dqs, 1):
        dq0 = dq0 + from_ring(part, TEAM - step).astype(F32)
    return dq0.astype(BF16), kv_grad[:, :E], kv_grad[:, E:]


def solution(mesh):
    fine = Mesh(
        mesh.devices.reshape(LINE // 2, 2, TEAM, 2, 2, 2, 2),
        ("quad", "pair", "ring", "core", "far_col", "near_col", "far"),
    )
    ctx = ("quad", "pair", "ring", "core")
    head = ("far_col", "near_col", "far")
    return jax.shard_map(
        per_device,
        mesh=fine,
        in_specs=(
            P(ctx, head), P(ctx, head), P(ctx, head), P(ctx, head),
            P(), P(), P(ctx), P(ctx + head),
        ),
        out_specs=(P(ctx, head), P(ctx, head), P(ctx, head)),
        check_vma=False,
    )
```

```python
import functools
import math

import jax
import jax.numpy as jnp
from jax import lax
from jax.experimental import pallas as pl
from jax.experimental.pallas import tpu as pltpu
from jax.sharding import Mesh, PartitionSpec as P

E = 128
GROUP = 6
HALF = 64
ROWS = 2 * HALF
TEAM = 4
LINE = 8
PARTS = LINE // 2
TILE = 4 * HALF
HEAD_COLS = TEAM * HALF
COLS = GROUP * HEAD_COLS
LAST = 2 * (LINE * TEAM * 2) - 1
NEG = -1e30
SCALE = 1.0 / math.sqrt(E)
SCALE2 = SCALE * math.log2(math.e)
LOG2E = math.log2(math.e)
F32 = jnp.float32
BF16 = jnp.bfloat16
I32 = jnp.int32
VMEM = 24 * 1024 * 1024


def dot(left, right, left_dim, right_dim):
    return lax.dot_general(
        left, right, (((left_dim,), (right_dim,)), ((), ())), preferred_element_type=F32
    )


def iota(shape, dim):
    return lax.broadcasted_iota(I32, shape, dim)


def call(kernel, outs, scratch=(), scalars=0, inputs=0, cost=None):
    spec = pl.BlockSpec(memory_space=pltpu.VMEM)
    return pl.pallas_call(
        kernel,
        out_shape=outs,
        in_specs=[pl.BlockSpec(memory_space=pltpu.SMEM)] * scalars + [spec] * inputs,
        out_specs=jax.tree.map(lambda _: spec, outs),
        scratch_shapes=list(scratch),
        compiler_params=pltpu.CompilerParams(vmem_limit_bytes=VMEM),
        cost_estimate=cost,
    )


def pack_kernel(
    where_ref, q_ref, slot_ref, length_ref, return_ref, out_ref, seg_ref
):
    line_place, core = where_ref[0], where_ref[2]
    width = GROUP * E
    out_ref[:ROWS, :] = q_ref[...]
    slot = slot_ref[...]
    row = iota((16, ROWS), 0)
    coded = jnp.where(row == 0, slot >> 7, jnp.where(row == 1, slot & 127, 0))
    out_ref[ROWS:, :] = jnp.zeros((16, width), BF16)
    out_ref[ROWS:, :ROWS] = coded.astype(F32).astype(BF16)

    lengths_row = length_ref[...].astype(F32)
    before = iota((E, E), 1) <= iota((E, E), 0)
    own = iota((E, E), 1) == iota((E, E), 0)
    ends = jnp.sum(jnp.where(before, lengths_row, 0.0), axis=1, keepdims=True)
    lengths = jnp.sum(jnp.where(own, lengths_row, 0.0), axis=1, keepdims=True)
    returns = jnp.sum(jnp.where(own, return_ref[...], 0.0), axis=1, keepdims=True)
    starts = ends - lengths
    column = iota((1, ROWS), 1)
    line = iota((8, ROWS), 0)
    block = jnp.zeros((8, ROWS), F32)
    for slot in range(TEAM):
        owner = 2 * (line_place * TEAM + slot) + core
        place_of = jnp.where(column < HALF, owner, LAST - owner)
        pos = (place_of * HALF + (column & 63)).astype(F32)
        inside = (pos >= starts) & (pos < ends)
        part = jnp.sum(jnp.where(inside, returns, 0.0), axis=0, keepdims=True)
        block = jnp.where(line == TEAM + slot, part, block)
    seg_ref[...] = block


def arrange(slots, refs, out_ref):
    for group in range(2):
        for head in range(GROUP):
            for ref, slot in zip(refs, slots):
                start = pl.multiple_of(head * HEAD_COLS + slot * HALF, HALF)
                out_ref[group, pl.ds(start, HALF), :] = ref[
                    group * HALF : (group + 1) * HALF, head * E : (head + 1) * E
                ]


def place(where_ref):
    z, ring, core = (where_ref[i] for i in range(3))
    return z, ring, core, [(ring - step) & 3 for step in range(TEAM)]


def causal_mask(group, z, ring, core):
    key_row = iota((TILE, 1), 0)
    piece = key_row >> 6
    key_owner = 2 * (((z & 6) + (piece & 1)) * TEAM + ring) + (core ^ (piece >> 1))
    column = iota((1, HEAD_COLS), 1)
    query_owner = 2 * (z * TEAM + (column >> 6)) + core
    if group == 1:
        key_owner, query_owner = LAST - key_owner, LAST - query_owner
    key_pos = key_owner * HALF + (key_row & 63)
    query_pos = query_owner * HALF + (column & 63)
    return key_pos <= query_pos


def free_visit(index, edge):
    wide = index < PARTS
    rest = index - PARTS
    early = rest < edge
    group = jnp.where(wide, 1, jnp.where(early, 0, 1))
    half = jnp.where(wide, 0, jnp.where(early, 0, 1))
    part = jnp.where(wide, index, jnp.where(early, rest, rest + 1))
    return group, half, part


def key_value_tile(kv_refs, half, part):
    rows = pl.ds(pl.multiple_of(half * HALF, HALF), HALF)
    pieces = [ref[pl.ds(part * 2, 2), rows, :].reshape(2 * HALF, 2 * E) for ref in kv_refs]
    return jnp.concatenate(pieces, axis=0)


def forward_kernel(
    where_ref, q0_ref, q1_ref, q2_ref, q3_ref, g0_ref, g1_ref, g2_ref, g3_ref, kv0_ref, kv1_ref,
    stat_ref, qs_ref, gs_ref, top_ref, sum_ref, term_ref,
):
    z, ring, core, slots = place(where_ref)
    arrange(slots, (q0_ref, q1_ref, q2_ref, q3_ref), qs_ref)
    arrange(slots, (g0_ref, g1_ref, g2_ref, g3_ref), gs_ref)
    kv_refs = (kv0_ref, kv1_ref)
    edge = z >> 1
    top_ref[...] = jnp.full(top_ref.shape, NEG, F32)
    sum_ref[...] = jnp.zeros(sum_ref.shape, F32)
    term_ref[...] = jnp.zeros(term_ref.shape, F32)

    def visit(group, half, part, mask):
        key_value = key_value_tile(kv_refs, half, part)
        key, value = key_value[:, :E], key_value[:, E:]
        for head in range(GROUP):
            cols = slice(head * HEAD_COLS, (head + 1) * HEAD_COLS)
            scores = dot(key, qs_ref[group, cols, :], 1, 1) * SCALE2
            dots = dot(value, gs_ref[group, cols, :], 1, 1)
            if mask is not None:
                scores = jnp.where(mask, scores, NEG)
            scores = scores.reshape(TILE // 8, 8, HEAD_COLS)
            dots = dots.reshape(TILE // 8, 8, HEAD_COLS)
            old = top_ref[group, :, cols]
            top = jnp.maximum(old, jnp.max(scores, axis=0))
            factor = jnp.exp2(old - top)
            prob = jnp.exp2(scores - top[None])
            top_ref[group, :, cols] = top
            sum_ref[group, :, cols] = factor * sum_ref[group, :, cols] + jnp.sum(prob, axis=0)
            term_ref[group, :, cols] = factor * term_ref[group, :, cols] + jnp.sum(
                prob * dots, axis=0
            )

    @pl.loop(0, 2 * PARTS - 1, unroll=True)
    def _(index):
        visit(*free_visit(index, edge), None)

    for group in range(2):
        visit(group, group, edge, causal_mask(group, z, ring, core))

    stat_ref[...] = jnp.zeros(stat_ref.shape, F32)
    for group in range(2):
        top = top_ref[group]
        best = jnp.max(top, axis=0, keepdims=True)
        factor = jnp.exp2(top - best)
        stat_ref[3 * group : 3 * group + 1, :] = best
        stat_ref[3 * group + 1 : 3 * group + 2, :] = jnp.sum(
            factor * sum_ref[group], axis=0, keepdims=True
        )
        stat_ref[3 * group + 2 : 3 * group + 3, :] = jnp.sum(
            factor * term_ref[group], axis=0, keepdims=True
        )


def lookup_kernel(
    where_ref, q0_ref, q1_ref, q2_ref, q3_ref, stat_ref, table_ref, seg_ref, out_ref
):
    z, ring, core, slots = place(where_ref)
    refs = (q0_ref, q1_ref, q2_ref, q3_ref)
    table = table_ref[:, 0, :]
    high = table.astype(BF16)
    rest = table - high.astype(F32)
    middle = rest.astype(BF16)
    low = (rest - middle.astype(F32)).astype(BF16)
    lane = iota((E, ROWS), 0)
    device = iota((2 * LINE, ROWS), 0)
    line = iota((8, ROWS), 0)
    block = seg_ref[...]
    for ref, slot in zip(refs, slots):
        code = ref[ROWS : ROWS + 16, :ROWS].astype(F32)
        owner = code[0:1].astype(I32)
        entry = code[1:2].astype(I32)
        pick = (lane == entry).astype(F32).astype(BF16)
        picked = dot(high, pick, 1, 0) + dot(middle, pick, 1, 0) + dot(low, pick, 1, 0)
        line_place = (owner >> 3) ^ jnp.where(((entry >> 4) & 1) == where_ref[3], 0, 4)
        row = jnp.where(((owner >> 1) & 3) == ring, line_place * 2 + (owner & 1), -1)
        part = jnp.sum(jnp.where(device == row, picked, 0.0), axis=0, keepdims=True)
        block = jnp.where(line == slot, part, block)
    for copy in range(TEAM):
        out_ref[copy] = stat_ref[...]
        for row in range(8):
            out_ref[copy, 6:7, row * ROWS : (row + 1) * ROWS] = block[row : row + 1]


def row_weights(stats):
    logw = [
        stats[0][6:7, (TEAM + s) * ROWS : (TEAM + s + 1) * ROWS]
        - sum(st[6:7, s * ROWS : (s + 1) * ROWS] for st in stats)
        for s in range(TEAM)
    ]
    low_lane = iota((1, ROWS), 1) < HALF
    groups = []
    for group in range(2):
        pieces = []
        for first in (0, 2):
            a, b = logw[first], logw[first + 1]
            if group == 0:
                b = pltpu.roll(jnp.broadcast_to(b, (8, ROWS)), HALF, 1)[0:1]
            else:
                a = pltpu.roll(jnp.broadcast_to(a, (8, ROWS)), HALF, 1)[0:1]
            pieces.append(jnp.where(low_lane, a, b))
        groups.append(jnp.concatenate(pieces, axis=1))
    return groups


def merge_stats(stat_ref, shift_ref, term_ref):
    stats = [stat_ref.at[s] for s in range(TEAM)]
    weights = row_weights(stats)
    for group in range(2):
        tops = [st[3 * group : 3 * group + 1, :] for st in stats]
        best = functools.reduce(jnp.maximum, tops)
        factors = [jnp.exp2(top - best) for top in tops]
        total = sum(f * st[3 * group + 1 : 3 * group + 2, :] for f, st in zip(factors, stats))
        term = sum(f * st[3 * group + 2 : 3 * group + 3, :] for f, st in zip(factors, stats))
        shift = best + jnp.log2(total)
        term_ref[group] = term / total
        for head in range(GROUP):
            cols = slice(head * HEAD_COLS, (head + 1) * HEAD_COLS)
            shift_ref[group, :, cols] = shift[:, cols] - weights[group] * LOG2E


def backward_kernel(
    where_ref, q0_ref, q1_ref, q2_ref, q3_ref, g0_ref, g1_ref, g2_ref, g3_ref, kv0_ref, kv1_ref, stat_ref,
    dkv0_ref, dkv1_ref, dq0_ref, dq1_ref, dq2_ref, dq3_ref,
    qs_ref, gs_ref, dqt_ref, acc_ref, shift_ref, term_ref, prob_ref, slope_ref, turn_ref,
):
    z, ring, core, slots = place(where_ref)
    kv_refs = (kv0_ref, kv1_ref)
    arrange(slots, (q0_ref, q1_ref, q2_ref, q3_ref), qs_ref)
    arrange(slots, (g0_ref, g1_ref, g2_ref, g3_ref), gs_ref)
    merge_stats(stat_ref, shift_ref, term_ref)
    acc_ref[...] = jnp.zeros(acc_ref.shape, F32)
    dqt_ref[...] = jnp.zeros(dqt_ref.shape, F32)
    edge, pair = z >> 1, z & 1

    def visit(group, half, part, mask):
        key_value = key_value_tile(kv_refs, half, part)
        key, value = key_value[:, :E], key_value[:, E:]
        for head in range(GROUP):
            cols = slice(head * HEAD_COLS, (head + 1) * HEAD_COLS)
            scores = dot(key, qs_ref[group, cols, :], 1, 1) * SCALE2
            dots = dot(value, gs_ref[group, cols, :], 1, 1)
            if mask is not None:
                scores = jnp.where(mask, scores, NEG)
            prob = jnp.exp2(scores - shift_ref[group, :, cols])
            prob_ref[:, cols] = prob.astype(BF16)
            slope_ref[:, cols] = (prob * (dots - term_ref[group, :, cols])).astype(BF16)
        slope = slope_ref[...]
        acc_ref[half, part, :, :E] += dot(slope, qs_ref[group], 1, 0)
        acc_ref[half, part, :, E:] += dot(prob_ref[...], gs_ref[group], 1, 0)
        dqt_ref[group] += dot(key, slope, 0, 0)

    @pl.loop(0, 2 * PARTS - 1, unroll=True)
    def _(index):
        visit(*free_visit(index, edge), None)

    for group in range(2):
        visit(group, group, edge, causal_mask(group, z, ring, core))

    scales = jnp.where(iota((1, 2 * E), 1) < E, SCALE, 1.0)
    for half in range(2):
        for part in range(PARTS):
            tile = (acc_ref[half, part] * scales).reshape(2, 2, HALF, 2 * E)
            rows = slice(half * HALF, (half + 1) * HALF)
            for piece in range(2):
                dkv0_ref[piece ^ pair, part, rows, :] = tile[0, piece]
                dkv1_ref[piece ^ pair, part, rows, :] = tile[1, piece].astype(BF16)
    targets = (dq0_ref, dq1_ref, dq2_ref, dq3_ref)
    for group in range(2):
        for head in range(GROUP):
            cols = slice(head * HEAD_COLS, (head + 1) * HEAD_COLS)
            turn_ref[...] = dqt_ref[group, :, cols].T * SCALE
            for ref, slot in zip(targets, slots):
                start = pl.multiple_of(slot * HALF, HALF)
                ref[group * HALF : (group + 1) * HALF, head * E : (head + 1) * E] = turn_ref[
                    pl.ds(start, HALF), :
                ].astype(ref.dtype)


def shape(dims, dtype):
    return jax.ShapeDtypeStruct(dims, dtype)


def swapped(x, axis):
    return lax.ppermute(x, axis, [(0, 1), (1, 0)])


def far_swapped(x):
    pairs = [(i, i ^ 5) for i in range(LINE)]
    return lax.ppermute(x, ("quad", "far"), pairs)


def from_ring(x, step):
    return lax.ppermute(x, "ring", [(i, (i + step) % TEAM) for i in range(TEAM)])


def per_device(queries, keys, values, cotangent, seg_lengths, seg_return, owner_slot, ref_term):
    head = lax.axis_index(("far_col", "near_col", "far"))
    place_names = (("quad", "pair"), "ring", "core", "far")
    where = jnp.stack([lax.axis_index(name) for name in place_names]).astype(I32)
    width = GROUP * E

    kv_own = jnp.broadcast_to(
        jnp.concatenate([keys, values], axis=1)[None], (LINE, ROWS, 2 * E)
    )
    q0, seg = call(
        pack_kernel,
        (shape((ROWS + 16, width), BF16), shape((8, E), F32)),
        scalars=1,
        inputs=4,
    )(
        where, queries, owner_slot.reshape(1, ROWS),
        seg_lengths.reshape(1, E), seg_return.reshape(1, E),
    )
    from_far = far_swapped(ref_term)
    lane = iota((8, E), 1) >> 4
    terms = jnp.where(lane == head, jnp.tile(ref_term, 8)[None], 0.0)
    terms = jnp.where(lane == (head ^ 1), jnp.tile(from_far, 8)[None], terms)
    kv_own, terms, q0 = lax.optimization_barrier((kv_own, terms, q0))
    kv0 = lax.all_to_all(kv_own, ("quad", "pair"), 0, 0, tiled=True)
    g0 = cotangent
    g3, q1 = from_ring(g0, 3), from_ring(q0, 1)
    q3, g1 = from_ring(q0, 3), from_ring(g0, 1)
    terms = terms + swapped(terms, "near_col")
    q1, g3, terms = lax.optimization_barrier((q1, g3, terms))
    q2, g2 = from_ring(q1, 1), from_ring(g3, 3)
    terms = terms + swapped(terms, "far_col")
    kv0, terms, q1, q2, q3, g1, g2, g3 = lax.optimization_barrier(
        (kv0, terms, q1, q2, q3, g1, g2, g3)
    )
    kv1 = swapped(kv0, "core")
    qs, gs = (q0, q1, q2, q3), (g0, g1, g2, g3)
    table = lax.all_to_all(
        jnp.broadcast_to(terms[None], (2 * LINE, 8, E)), ("quad", "pair", "core"), 0, 0, tiled=True
    )
    pairs = 9 * TILE * COLS
    kv_scratch = [pltpu.VMEM((2, COLS, E), BF16), pltpu.VMEM((2, COLS, E), BF16)]
    stat = call(
        forward_kernel,
        shape((8, COLS), F32),
        kv_scratch + [pltpu.VMEM((2, 8, COLS), F32)] * 3,
        scalars=1,
        inputs=10,
        cost=pl.CostEstimate(flops=4 * E * pairs, bytes_accessed=4 << 20, transcendentals=pairs),
    )(where, *qs, *gs, kv0, kv1)
    stat = call(lookup_kernel, shape((TEAM, 8, COLS), F32), scalars=1, inputs=7)(
        where, *qs, stat, table, seg
    )
    stats = lax.all_to_all(stat, "ring", 0, 0, tiled=True)
    core_grad = (2, LINE // 2, ROWS, 2 * E)
    query_grad = shape((ROWS, width), BF16)
    grad0, grad1, dq0, *dqs = call(
        backward_kernel,
        (
            shape(core_grad, F32), shape(core_grad, BF16), shape((ROWS, width), F32),
            query_grad, query_grad, query_grad,
        ),
        kv_scratch
        + [
            pltpu.VMEM((2, E, COLS), F32),
            pltpu.VMEM((2, PARTS, TILE, 2 * E), F32),
            pltpu.VMEM((2, 1, COLS), F32),
            pltpu.VMEM((2, 1, COLS), F32),
            pltpu.VMEM((TILE, COLS), BF16),
            pltpu.VMEM((TILE, COLS), BF16),
            pltpu.VMEM((HEAD_COLS, E), F32),
        ],
        scalars=1,
        inputs=11,
        cost=pl.CostEstimate(flops=10 * E * pairs, bytes_accessed=5 << 20, transcendentals=pairs),
    )(where, *qs, *gs, kv0, kv1, stats)

    own = grad0 + swapped(grad1, "core").astype(F32)
    parts = (own[0] + swapped(own[1].astype(BF16), "pair").astype(F32)).astype(BF16)
    parts = lax.all_to_all(parts, "quad", 0, 0, tiled=True)
    kv_grad = jnp.sum(parts.astype(F32), axis=0).astype(BF16)

    for step, part in enumerate(dqs, 1):
        dq0 = dq0 + from_ring(part, TEAM - step).astype(F32)
    return dq0.astype(BF16), kv_grad[:, :E], kv_grad[:, E:]


def solution(mesh):
    fine = Mesh(
        mesh.devices.reshape(LINE // 2, 2, TEAM, 2, 2, 2, 2),
        ("quad", "pair", "ring", "core", "far_col", "near_col", "far"),
    )
    ctx = ("quad", "pair", "ring", "core")
    head = ("far_col", "near_col", "far")
    return jax.shard_map(
        per_device,
        mesh=fine,
        in_specs=(
            P(ctx, head), P(ctx, head), P(ctx, head), P(ctx, head),
            P(), P(), P(ctx), P(ctx + head),
        ),
        out_specs=(P(ctx, head), P(ctx, head), P(ctx, head)),
        check_vma=False,
    )
```

```python
import functools
import math

import jax
import jax.numpy as jnp
from jax import lax
from jax.experimental import pallas as pl
from jax.experimental.pallas import tpu as pltpu
from jax.sharding import Mesh, PartitionSpec as P

E = 128
GROUP = 6
HALF = 64
ROWS = 2 * HALF
TEAM = 4
LINE = 8
PARTS = LINE // 2
TILE = 4 * HALF
HEAD_COLS = TEAM * HALF
COLS = GROUP * HEAD_COLS
LAST = 2 * (LINE * TEAM * 2) - 1
NEG = -1e30
SCALE = 1.0 / math.sqrt(E)
SCALE2 = SCALE * math.log2(math.e)
LOG2E = math.log2(math.e)
F32 = jnp.float32
BF16 = jnp.bfloat16
I32 = jnp.int32
VMEM = 24 * 1024 * 1024


def dot(left, right, left_dim, right_dim):
    return lax.dot_general(
        left, right, (((left_dim,), (right_dim,)), ((), ())), preferred_element_type=F32
    )


def iota(shape, dim):
    return lax.broadcasted_iota(I32, shape, dim)


def call(kernel, outs, scratch=(), scalars=0, inputs=0, cost=None):
    spec = pl.BlockSpec(memory_space=pltpu.VMEM)
    return pl.pallas_call(
        kernel,
        out_shape=outs,
        in_specs=[pl.BlockSpec(memory_space=pltpu.SMEM)] * scalars + [spec] * inputs,
        out_specs=jax.tree.map(lambda _: spec, outs),
        scratch_shapes=list(scratch),
        compiler_params=pltpu.CompilerParams(vmem_limit_bytes=VMEM),
        cost_estimate=cost,
    )


def pack_kernel(
    where_ref, q_ref, g_ref, slot_ref, length_ref, return_ref, out_ref, seg_ref
):
    line_place, core = where_ref[0], where_ref[2]
    width = GROUP * E
    out_ref[0, :ROWS, :] = q_ref[...]
    out_ref[1, :ROWS, :] = g_ref[...]
    slot = slot_ref[...]
    row = iota((16, ROWS), 0)
    coded = jnp.where(row == 0, slot >> 7, jnp.where(row == 1, slot & 127, 0))
    out_ref[:, ROWS:, :] = jnp.zeros((2, 16, width), BF16)
    out_ref[0, ROWS:, :ROWS] = coded.astype(F32).astype(BF16)

    lengths_row = length_ref[...].astype(F32)
    before = iota((E, E), 1) <= iota((E, E), 0)
    own = iota((E, E), 1) == iota((E, E), 0)
    ends = jnp.sum(jnp.where(before, lengths_row, 0.0), axis=1, keepdims=True)
    lengths = jnp.sum(jnp.where(own, lengths_row, 0.0), axis=1, keepdims=True)
    returns = jnp.sum(jnp.where(own, return_ref[...], 0.0), axis=1, keepdims=True)
    starts = ends - lengths
    column = iota((1, ROWS), 1)
    line = iota((8, ROWS), 0)
    block = jnp.zeros((8, ROWS), F32)
    for slot in range(TEAM):
        owner = 2 * (line_place * TEAM + slot) + core
        place_of = jnp.where(column < HALF, owner, LAST - owner)
        pos = (place_of * HALF + (column & 63)).astype(F32)
        inside = (pos >= starts) & (pos < ends)
        part = jnp.sum(jnp.where(inside, returns, 0.0), axis=0, keepdims=True)
        block = jnp.where(line == TEAM + slot, part, block)
    seg_ref[...] = block


def arrange(slots, refs, out_ref):
    for group in range(2):
        for head in range(GROUP):
            for ref, slot in zip(refs, slots):
                start = pl.multiple_of(head * HEAD_COLS + slot * HALF, HALF)
                out_ref[group, pl.ds(start, HALF), :] = ref[
                    group * HALF : (group + 1) * HALF, head * E : (head + 1) * E
                ]


def place(where_ref):
    z, ring, core = (where_ref[i] for i in range(3))
    return z, ring, core, [(ring - step) & 3 for step in range(TEAM)]


def causal_mask(group, z, ring, core):
    key_row = iota((TILE, 1), 0)
    piece = key_row >> 6
    key_owner = 2 * (((z & 6) + (piece & 1)) * TEAM + ring) + (core ^ (piece >> 1))
    column = iota((1, HEAD_COLS), 1)
    query_owner = 2 * (z * TEAM + (column >> 6)) + core
    if group == 1:
        key_owner, query_owner = LAST - key_owner, LAST - query_owner
    key_pos = key_owner * HALF + (key_row & 63)
    query_pos = query_owner * HALF + (column & 63)
    return key_pos <= query_pos


def free_visit(index, edge):
    wide = index < PARTS
    rest = index - PARTS
    early = rest < edge
    group = jnp.where(wide, 1, jnp.where(early, 0, 1))
    half = jnp.where(wide, 0, jnp.where(early, 0, 1))
    part = jnp.where(wide, index, jnp.where(early, rest, rest + 1))
    return group, half, part


def key_value_tile(kv_refs, half, part):
    rows = pl.ds(pl.multiple_of(half * HALF, HALF), HALF)
    pieces = [ref[pl.ds(part * 2, 2), rows, :].reshape(2 * HALF, 2 * E) for ref in kv_refs]
    return jnp.concatenate(pieces, axis=0)


def forward_kernel(
    where_ref, qg0_ref, qg1_ref, qg2_ref, qg3_ref, kv0_ref, kv1_ref,
    stat_ref, qs_ref, gs_ref, top_ref, sum_ref, term_ref,
):
    z, ring, core, slots = place(where_ref)
    refs = (qg0_ref, qg1_ref, qg2_ref, qg3_ref)
    arrange(slots, [ref.at[0] for ref in refs], qs_ref)
    arrange(slots, [ref.at[1] for ref in refs], gs_ref)
    kv_refs = (kv0_ref, kv1_ref)
    edge = z >> 1
    top_ref[...] = jnp.full(top_ref.shape, NEG, F32)
    sum_ref[...] = jnp.zeros(sum_ref.shape, F32)
    term_ref[...] = jnp.zeros(term_ref.shape, F32)

    def visit(group, half, part, mask):
        key_value = key_value_tile(kv_refs, half, part)
        key, value = key_value[:, :E], key_value[:, E:]
        for head in range(GROUP):
            cols = slice(head * HEAD_COLS, (head + 1) * HEAD_COLS)
            scores = dot(key, qs_ref[group, cols, :], 1, 1) * SCALE2
            dots = dot(value, gs_ref[group, cols, :], 1, 1)
            if mask is not None:
                scores = jnp.where(mask, scores, NEG)
            scores = scores.reshape(TILE // 8, 8, HEAD_COLS)
            dots = dots.reshape(TILE // 8, 8, HEAD_COLS)
            old = top_ref[group, :, cols]
            top = jnp.maximum(old, jnp.max(scores, axis=0))
            factor = jnp.exp2(old - top)
            prob = jnp.exp2(scores - top[None])
            top_ref[group, :, cols] = top
            sum_ref[group, :, cols] = factor * sum_ref[group, :, cols] + jnp.sum(prob, axis=0)
            term_ref[group, :, cols] = factor * term_ref[group, :, cols] + jnp.sum(
                prob * dots, axis=0
            )

    @pl.loop(0, 2 * PARTS - 1, unroll=True)
    def _(index):
        visit(*free_visit(index, edge), None)

    for group in range(2):
        visit(group, group, edge, causal_mask(group, z, ring, core))

    stat_ref[...] = jnp.zeros(stat_ref.shape, F32)
    for group in range(2):
        top = top_ref[group]
        best = jnp.max(top, axis=0, keepdims=True)
        factor = jnp.exp2(top - best)
        stat_ref[3 * group : 3 * group + 1, :] = best
        stat_ref[3 * group + 1 : 3 * group + 2, :] = jnp.sum(
            factor * sum_ref[group], axis=0, keepdims=True
        )
        stat_ref[3 * group + 2 : 3 * group + 3, :] = jnp.sum(
            factor * term_ref[group], axis=0, keepdims=True
        )


def lookup_kernel(
    where_ref, qg0_ref, qg1_ref, qg2_ref, qg3_ref, stat_ref, table_ref, seg_ref, out_ref
):
    z, ring, core, slots = place(where_ref)
    refs = [ref.at[0] for ref in (qg0_ref, qg1_ref, qg2_ref, qg3_ref)]
    table = table_ref[:, 0, :]
    high = table.astype(BF16)
    rest = table - high.astype(F32)
    middle = rest.astype(BF16)
    low = (rest - middle.astype(F32)).astype(BF16)
    lane = iota((E, ROWS), 0)
    device = iota((2 * LINE, ROWS), 0)
    line = iota((8, ROWS), 0)
    block = seg_ref[...]
    for ref, slot in zip(refs, slots):
        code = ref[ROWS : ROWS + 16, :ROWS].astype(F32)
        owner = code[0:1].astype(I32)
        entry = code[1:2].astype(I32)
        pick = (lane == entry).astype(F32).astype(BF16)
        picked = dot(high, pick, 1, 0) + dot(middle, pick, 1, 0) + dot(low, pick, 1, 0)
        line_place = (owner >> 3) ^ jnp.where(((entry >> 4) & 1) == where_ref[3], 0, 4)
        row = jnp.where(((owner >> 1) & 3) == ring, line_place * 2 + (owner & 1), -1)
        part = jnp.sum(jnp.where(device == row, picked, 0.0), axis=0, keepdims=True)
        block = jnp.where(line == slot, part, block)
    for copy in range(TEAM):
        out_ref[copy] = stat_ref[...]
        for row in range(8):
            out_ref[copy, 6:7, row * ROWS : (row + 1) * ROWS] = block[row : row + 1]


def row_weights(stats):
    logw = [
        stats[0][6:7, (TEAM + s) * ROWS : (TEAM + s + 1) * ROWS]
        - sum(st[6:7, s * ROWS : (s + 1) * ROWS] for st in stats)
        for s in range(TEAM)
    ]
    low_lane = iota((1, ROWS), 1) < HALF
    groups = []
    for group in range(2):
        pieces = []
        for first in (0, 2):
            a, b = logw[first], logw[first + 1]
            if group == 0:
                b = pltpu.roll(jnp.broadcast_to(b, (8, ROWS)), HALF, 1)[0:1]
            else:
                a = pltpu.roll(jnp.broadcast_to(a, (8, ROWS)), HALF, 1)[0:1]
            pieces.append(jnp.where(low_lane, a, b))
        groups.append(jnp.concatenate(pieces, axis=1))
    return groups


def merge_stats(stat_ref, shift_ref, term_ref):
    stats = [stat_ref.at[s] for s in range(TEAM)]
    weights = row_weights(stats)
    for group in range(2):
        tops = [st[3 * group : 3 * group + 1, :] for st in stats]
        best = functools.reduce(jnp.maximum, tops)
        factors = [jnp.exp2(top - best) for top in tops]
        total = sum(f * st[3 * group + 1 : 3 * group + 2, :] for f, st in zip(factors, stats))
        term = sum(f * st[3 * group + 2 : 3 * group + 3, :] for f, st in zip(factors, stats))
        shift = best + jnp.log2(total)
        term_ref[group] = term / total
        for head in range(GROUP):
            cols = slice(head * HEAD_COLS, (head + 1) * HEAD_COLS)
            shift_ref[group, :, cols] = shift[:, cols] - weights[group] * LOG2E


def backward_kernel(
    where_ref, qg0_ref, qg1_ref, qg2_ref, qg3_ref, kv0_ref, kv1_ref, stat_ref,
    dkv0_ref, dkv1_ref, dq0_ref, dq1_ref, dq2_ref, dq3_ref,
    qs_ref, gs_ref, dqt_ref, acc_ref, shift_ref, term_ref, prob_ref, slope_ref, turn_ref,
):
    z, ring, core, slots = place(where_ref)
    kv_refs = (kv0_ref, kv1_ref)
    refs = (qg0_ref, qg1_ref, qg2_ref, qg3_ref)
    arrange(slots, [ref.at[0] for ref in refs], qs_ref)
    arrange(slots, [ref.at[1] for ref in refs], gs_ref)
    merge_stats(stat_ref, shift_ref, term_ref)
    acc_ref[...] = jnp.zeros(acc_ref.shape, F32)
    dqt_ref[...] = jnp.zeros(dqt_ref.shape, F32)
    edge, pair = z >> 1, z & 1

    def visit(group, half, part, mask):
        key_value = key_value_tile(kv_refs, half, part)
        key, value = key_value[:, :E], key_value[:, E:]
        for head in range(GROUP):
            cols = slice(head * HEAD_COLS, (head + 1) * HEAD_COLS)
            scores = dot(key, qs_ref[group, cols, :], 1, 1) * SCALE2
            dots = dot(value, gs_ref[group, cols, :], 1, 1)
            if mask is not None:
                scores = jnp.where(mask, scores, NEG)
            prob = jnp.exp2(scores - shift_ref[group, :, cols])
            prob_ref[:, cols] = prob.astype(BF16)
            slope_ref[:, cols] = (prob * (dots - term_ref[group, :, cols])).astype(BF16)
        slope = slope_ref[...]
        acc_ref[half, part, :, :E] += dot(slope, qs_ref[group], 1, 0)
        acc_ref[half, part, :, E:] += dot(prob_ref[...], gs_ref[group], 1, 0)
        dqt_ref[group] += dot(key, slope, 0, 0)

    @pl.loop(0, 2 * PARTS - 1, unroll=True)
    def _(index):
        visit(*free_visit(index, edge), None)

    for group in range(2):
        visit(group, group, edge, causal_mask(group, z, ring, core))

    scales = jnp.where(iota((1, 2 * E), 1) < E, SCALE, 1.0)
    for half in range(2):
        for part in range(PARTS):
            tile = (acc_ref[half, part] * scales).reshape(2, 2, HALF, 2 * E)
            rows = slice(half * HALF, (half + 1) * HALF)
            for piece in range(2):
                dkv0_ref[piece ^ pair, part, rows, :] = tile[0, piece]
                dkv1_ref[piece ^ pair, part, rows, :] = tile[1, piece].astype(BF16)
    targets = (dq0_ref, dq1_ref, dq2_ref, dq3_ref)
    for group in range(2):
        for head in range(GROUP):
            cols = slice(head * HEAD_COLS, (head + 1) * HEAD_COLS)
            turn_ref[...] = dqt_ref[group, :, cols].T * SCALE
            for ref, slot in zip(targets, slots):
                start = pl.multiple_of(slot * HALF, HALF)
                ref[group * HALF : (group + 1) * HALF, head * E : (head + 1) * E] = turn_ref[
                    pl.ds(start, HALF), :
                ].astype(ref.dtype)


def shape(dims, dtype):
    return jax.ShapeDtypeStruct(dims, dtype)


def swapped(x, axis):
    return lax.ppermute(x, axis, [(0, 1), (1, 0)])


def far_swapped(x):
    pairs = [(i, i ^ 5) for i in range(LINE)]
    return lax.ppermute(x, ("quad", "far"), pairs)


def from_ring(x, step):
    return lax.ppermute(x, "ring", [(i, (i + step) % TEAM) for i in range(TEAM)])


def per_device(queries, keys, values, cotangent, seg_lengths, seg_return, owner_slot, ref_term):
    head = lax.axis_index(("far_col", "near_col", "far"))
    place_names = (("quad", "pair"), "ring", "core", "far")
    where = jnp.stack([lax.axis_index(name) for name in place_names]).astype(I32)
    width = GROUP * E

    kv_own = jnp.concatenate(
        [jnp.broadcast_to(x[None], (LINE, ROWS, E)) for x in (keys, values)], axis=2
    )
    qg0, seg = call(
        pack_kernel,
        (shape((2, ROWS + 16, width), BF16), shape((8, E), F32)),
        scalars=1,
        inputs=5,
    )(
        where, queries, cotangent, owner_slot.reshape(1, ROWS),
        seg_lengths.reshape(1, E), seg_return.reshape(1, E),
    )
    from_far = far_swapped(ref_term)
    lane = iota((8, E), 1) >> 4
    terms = jnp.where(lane == head, jnp.tile(ref_term, 8)[None], 0.0)
    terms = jnp.where(lane == (head ^ 1), jnp.tile(from_far, 8)[None], terms)
    kv_own, terms, qg0 = lax.optimization_barrier((kv_own, terms, qg0))
    kv0 = lax.all_to_all(kv_own, ("quad", "pair"), 0, 0, tiled=True)
    qg1, qg3 = from_ring(qg0, 1), from_ring(qg0, 3)
    terms = terms + swapped(terms, "near_col")
    qg1, terms = lax.optimization_barrier((qg1, terms))
    qg2 = from_ring(qg1, 1)
    terms = terms + swapped(terms, "far_col")
    kv0, terms, qg1, qg2, qg3 = lax.optimization_barrier((kv0, terms, qg1, qg2, qg3))
    team = (qg0, qg1, qg2, qg3)
    kv1 = swapped(kv0, "core")
    table = lax.all_to_all(
        jnp.broadcast_to(terms[None], (2 * LINE, 8, E)), ("quad", "pair", "core"), 0, 0, tiled=True
    )
    pairs = 9 * TILE * COLS
    kv_scratch = [pltpu.VMEM((2, COLS, E), BF16), pltpu.VMEM((2, COLS, E), BF16)]
    stat = call(
        forward_kernel,
        shape((8, COLS), F32),
        kv_scratch + [pltpu.VMEM((2, 8, COLS), F32)] * 3,
        scalars=1,
        inputs=6,
        cost=pl.CostEstimate(flops=4 * E * pairs, bytes_accessed=4 << 20, transcendentals=pairs),
    )(where, *team, kv0, kv1)
    stat = call(lookup_kernel, shape((TEAM, 8, COLS), F32), scalars=1, inputs=7)(
        where, *team, stat, table, seg
    )
    stats = lax.all_to_all(stat, "ring", 0, 0, tiled=True)
    core_grad = (2, LINE // 2, ROWS, 2 * E)
    query_grad = shape((ROWS, width), BF16)
    grad0, grad1, dq0, *dqs = call(
        backward_kernel,
        (
            shape(core_grad, F32), shape(core_grad, BF16), shape((ROWS, width), F32),
            query_grad, query_grad, query_grad,
        ),
        kv_scratch
        + [
            pltpu.VMEM((2, E, COLS), F32),
            pltpu.VMEM((2, PARTS, TILE, 2 * E), F32),
            pltpu.VMEM((2, 1, COLS), F32),
            pltpu.VMEM((2, 1, COLS), F32),
            pltpu.VMEM((TILE, COLS), BF16),
            pltpu.VMEM((TILE, COLS), BF16),
            pltpu.VMEM((HEAD_COLS, E), F32),
        ],
        scalars=1,
        inputs=7,
        cost=pl.CostEstimate(flops=10 * E * pairs, bytes_accessed=5 << 20, transcendentals=pairs),
    )(where, *team, kv0, kv1, stats)

    own = grad0 + swapped(grad1, "core").astype(F32)
    parts = (own[0] + swapped(own[1].astype(BF16), "pair").astype(F32)).astype(BF16)
    parts = lax.all_to_all(parts, "quad", 0, 0, tiled=True)
    kv_grad = jnp.sum(parts.astype(F32), axis=0).astype(BF16)

    for step, part in enumerate(dqs, 1):
        dq0 = dq0 + from_ring(part, TEAM - step).astype(F32)
    return dq0.astype(BF16), kv_grad[:, :E], kv_grad[:, E:]


def solution(mesh):
    fine = Mesh(
        mesh.devices.reshape(LINE // 2, 2, TEAM, 2, 2, 2, 2),
        ("quad", "pair", "ring", "core", "far_col", "near_col", "far"),
    )
    ctx = ("quad", "pair", "ring", "core")
    head = ("far_col", "near_col", "far")
    return jax.shard_map(
        per_device,
        mesh=fine,
        in_specs=(
            P(ctx, head), P(ctx, head), P(ctx, head), P(ctx, head),
            P(), P(), P(ctx), P(ctx + head),
        ),
        out_specs=(P(ctx, head), P(ctx, head), P(ctx, head)),
        check_vma=False,
    )
```

```python
import functools
import math

import jax
import jax.numpy as jnp
from jax import lax
from jax.experimental import pallas as pl
from jax.experimental.pallas import tpu as pltpu
from jax.sharding import Mesh, PartitionSpec as P

E = 128
GROUP = 6
HALF = 64
ROWS = 2 * HALF
TEAM = 4
LINE = 8
PARTS = LINE // 2
TILE = 4 * HALF
HEAD_COLS = TEAM * HALF
COLS = GROUP * HEAD_COLS
LAST = 2 * (LINE * TEAM * 2) - 1
NEG = -1e30
SCALE = 1.0 / math.sqrt(E)
SCALE2 = SCALE * math.log2(math.e)
LOG2E = math.log2(math.e)
F32 = jnp.float32
BF16 = jnp.bfloat16
I32 = jnp.int32
VMEM = 24 * 1024 * 1024


def dot(left, right, left_dim, right_dim):
    return lax.dot_general(
        left, right, (((left_dim,), (right_dim,)), ((), ())), preferred_element_type=F32
    )


def iota(shape, dim):
    return lax.broadcasted_iota(I32, shape, dim)


def call(kernel, outs, scratch=(), scalars=0, inputs=0, cost=None):
    spec = pl.BlockSpec(memory_space=pltpu.VMEM)
    return pl.pallas_call(
        kernel,
        out_shape=outs,
        in_specs=[pl.BlockSpec(memory_space=pltpu.SMEM)] * scalars + [spec] * inputs,
        out_specs=jax.tree.map(lambda _: spec, outs),
        scratch_shapes=list(scratch),
        compiler_params=pltpu.CompilerParams(vmem_limit_bytes=VMEM),
        cost_estimate=cost,
    )


def pack_kernel(
    where_ref, q_ref, g_ref, slot_ref, length_ref, return_ref, out_ref, seg_ref
):
    line_place, core = where_ref[0], where_ref[2]
    width = GROUP * E
    out_ref[0, :ROWS, :] = q_ref[...]
    out_ref[1, :ROWS, :] = g_ref[...]
    slot = slot_ref[...]
    row = iota((16, ROWS), 0)
    coded = jnp.where(row == 0, slot >> 7, jnp.where(row == 1, slot & 127, 0))
    out_ref[:, ROWS:, :] = jnp.zeros((2, 16, width), BF16)
    out_ref[0, ROWS:, :ROWS] = coded.astype(F32).astype(BF16)

    lengths_row = length_ref[...].astype(F32)
    before = iota((E, E), 1) <= iota((E, E), 0)
    own = iota((E, E), 1) == iota((E, E), 0)
    ends = jnp.sum(jnp.where(before, lengths_row, 0.0), axis=1, keepdims=True)
    lengths = jnp.sum(jnp.where(own, lengths_row, 0.0), axis=1, keepdims=True)
    returns = jnp.sum(jnp.where(own, return_ref[...], 0.0), axis=1, keepdims=True)
    starts = ends - lengths
    column = iota((1, ROWS), 1)
    line = iota((8, ROWS), 0)
    block = jnp.zeros((8, ROWS), F32)
    for slot in range(TEAM):
        owner = 2 * (line_place * TEAM + slot) + core
        place_of = jnp.where(column < HALF, owner, LAST - owner)
        pos = (place_of * HALF + (column & 63)).astype(F32)
        inside = (pos >= starts) & (pos < ends)
        part = jnp.sum(jnp.where(inside, returns, 0.0), axis=0, keepdims=True)
        block = jnp.where(line == TEAM + slot, part, block)
    seg_ref[...] = block


def arrange(slots, refs, out_ref):
    for group in range(2):
        for head in range(GROUP):
            for ref, slot in zip(refs, slots):
                start = pl.multiple_of(head * HEAD_COLS + slot * HALF, HALF)
                out_ref[group, pl.ds(start, HALF), :] = ref[
                    group * HALF : (group + 1) * HALF, head * E : (head + 1) * E
                ]


def place(where_ref):
    z, ring, core = (where_ref[i] for i in range(3))
    return z, ring, core, [(ring - step) & 3 for step in range(TEAM)]


def causal_mask(group, z, ring, core):
    key_row = iota((TILE, 1), 0)
    piece = key_row >> 6
    key_owner = 2 * (((z & 6) + (piece & 1)) * TEAM + ring) + (core ^ (piece >> 1))
    column = iota((1, HEAD_COLS), 1)
    query_owner = 2 * (z * TEAM + (column >> 6)) + core
    if group == 1:
        key_owner, query_owner = LAST - key_owner, LAST - query_owner
    key_pos = key_owner * HALF + (key_row & 63)
    query_pos = query_owner * HALF + (column & 63)
    return key_pos <= query_pos


def free_visit(index, edge):
    wide = index < PARTS
    rest = index - PARTS
    early = rest < edge
    group = jnp.where(wide, 1, jnp.where(early, 0, 1))
    half = jnp.where(wide, 0, jnp.where(early, 0, 1))
    part = jnp.where(wide, index, jnp.where(early, rest, rest + 1))
    return group, half, part


def key_value_tile(kv_refs, half, part):
    rows = pl.ds(pl.multiple_of(half * HALF, HALF), HALF)
    pieces = [ref[pl.ds(part * 2, 2), rows, :].reshape(2 * HALF, 2 * E) for ref in kv_refs]
    return jnp.concatenate(pieces, axis=0)


def forward_kernel(
    where_ref, qg0_ref, qg1_ref, qg2_ref, qg3_ref, kv0_ref, kv1_ref,
    stat_ref, qs_ref, gs_ref, top_ref, sum_ref, term_ref,
):
    z, ring, core, slots = place(where_ref)
    refs = (qg0_ref, qg1_ref, qg2_ref, qg3_ref)
    arrange(slots, [ref.at[0] for ref in refs], qs_ref)
    arrange(slots, [ref.at[1] for ref in refs], gs_ref)
    kv_refs = (kv0_ref, kv1_ref)
    edge = z >> 1
    top_ref[...] = jnp.full(top_ref.shape, NEG, F32)
    sum_ref[...] = jnp.zeros(sum_ref.shape, F32)
    term_ref[...] = jnp.zeros(term_ref.shape, F32)

    def visit(group, half, part, mask):
        key_value = key_value_tile(kv_refs, half, part)
        key, value = key_value[:, :E], key_value[:, E:]
        for head in range(GROUP):
            cols = slice(head * HEAD_COLS, (head + 1) * HEAD_COLS)
            scores = dot(key, qs_ref[group, cols, :], 1, 1) * SCALE2
            dots = dot(value, gs_ref[group, cols, :], 1, 1)
            if mask is not None:
                scores = jnp.where(mask, scores, NEG)
            scores = scores.reshape(TILE // 8, 8, HEAD_COLS)
            dots = dots.reshape(TILE // 8, 8, HEAD_COLS)
            old = top_ref[group, :, cols]
            top = jnp.maximum(old, jnp.max(scores, axis=0))
            factor = jnp.exp2(old - top)
            prob = jnp.exp2(scores - top[None])
            top_ref[group, :, cols] = top
            sum_ref[group, :, cols] = factor * sum_ref[group, :, cols] + jnp.sum(prob, axis=0)
            term_ref[group, :, cols] = factor * term_ref[group, :, cols] + jnp.sum(
                prob * dots, axis=0
            )

    @pl.loop(0, 2 * PARTS - 1, unroll=True)
    def _(index):
        visit(*free_visit(index, edge), None)

    for group in range(2):
        visit(group, group, edge, causal_mask(group, z, ring, core))

    stat_ref[...] = jnp.zeros(stat_ref.shape, F32)
    for group in range(2):
        top = top_ref[group]
        best = jnp.max(top, axis=0, keepdims=True)
        factor = jnp.exp2(top - best)
        stat_ref[3 * group : 3 * group + 1, :] = best
        stat_ref[3 * group + 1 : 3 * group + 2, :] = jnp.sum(
            factor * sum_ref[group], axis=0, keepdims=True
        )
        stat_ref[3 * group + 2 : 3 * group + 3, :] = jnp.sum(
            factor * term_ref[group], axis=0, keepdims=True
        )


def lookup_kernel(
    where_ref, qg0_ref, qg1_ref, qg2_ref, qg3_ref, stat_ref, table_ref, seg_ref, out_ref
):
    z, ring, core, slots = place(where_ref)
    refs = [ref.at[0] for ref in (qg0_ref, qg1_ref, qg2_ref, qg3_ref)]
    table = table_ref[:, 0, :]
    high = table.astype(BF16)
    rest = table - high.astype(F32)
    middle = rest.astype(BF16)
    low = (rest - middle.astype(F32)).astype(BF16)
    lane = iota((E, ROWS), 0)
    device = iota((2 * LINE, ROWS), 0)
    line = iota((8, ROWS), 0)
    block = seg_ref[...]
    for ref, slot in zip(refs, slots):
        code = ref[ROWS : ROWS + 16, :ROWS].astype(F32)
        owner = code[0:1].astype(I32)
        entry = code[1:2].astype(I32)
        pick = (lane == entry).astype(F32).astype(BF16)
        picked = dot(high, pick, 1, 0) + dot(middle, pick, 1, 0) + dot(low, pick, 1, 0)
        line_place = (owner >> 3) ^ jnp.where(((entry >> 4) & 1) == where_ref[3], 0, 4)
        row = jnp.where(((owner >> 1) & 3) == ring, line_place * 2 + (owner & 1), -1)
        part = jnp.sum(jnp.where(device == row, picked, 0.0), axis=0, keepdims=True)
        block = jnp.where(line == slot, part, block)
    for copy in range(TEAM):
        out_ref[copy] = stat_ref[...]
        for row in range(8):
            out_ref[copy, 6:7, row * ROWS : (row + 1) * ROWS] = block[row : row + 1]


def row_weights(stats):
    logw = [
        stats[0][6:7, (TEAM + s) * ROWS : (TEAM + s + 1) * ROWS]
        - sum(st[6:7, s * ROWS : (s + 1) * ROWS] for st in stats)
        for s in range(TEAM)
    ]
    low_lane = iota((1, ROWS), 1) < HALF
    groups = []
    for group in range(2):
        pieces = []
        for first in (0, 2):
            a, b = logw[first], logw[first + 1]
            if group == 0:
                b = pltpu.roll(jnp.broadcast_to(b, (8, ROWS)), HALF, 1)[0:1]
            else:
                a = pltpu.roll(jnp.broadcast_to(a, (8, ROWS)), HALF, 1)[0:1]
            pieces.append(jnp.where(low_lane, a, b))
        groups.append(jnp.concatenate(pieces, axis=1))
    return groups


def merge_stats(stat_ref, shift_ref, term_ref):
    stats = [stat_ref.at[s] for s in range(TEAM)]
    weights = row_weights(stats)
    for group in range(2):
        tops = [st[3 * group : 3 * group + 1, :] for st in stats]
        best = functools.reduce(jnp.maximum, tops)
        factors = [jnp.exp2(top - best) for top in tops]
        total = sum(f * st[3 * group + 1 : 3 * group + 2, :] for f, st in zip(factors, stats))
        term = sum(f * st[3 * group + 2 : 3 * group + 3, :] for f, st in zip(factors, stats))
        shift = best + jnp.log2(total)
        term_ref[group] = term / total
        for head in range(GROUP):
            cols = slice(head * HEAD_COLS, (head + 1) * HEAD_COLS)
            shift_ref[group, :, cols] = shift[:, cols] - weights[group] * LOG2E


def backward_kernel(
    where_ref, qg0_ref, qg1_ref, qg2_ref, qg3_ref, kv0_ref, kv1_ref, stat_ref,
    dkv0_ref, dkv1_ref, dq0_ref, dq1_ref, dq2_ref, dq3_ref,
    qs_ref, gs_ref, dqt_ref, acc_ref, shift_ref, term_ref, prob_ref, slope_ref, turn_ref,
):
    z, ring, core, slots = place(where_ref)
    kv_refs = (kv0_ref, kv1_ref)
    refs = (qg0_ref, qg1_ref, qg2_ref, qg3_ref)
    arrange(slots, [ref.at[0] for ref in refs], qs_ref)
    arrange(slots, [ref.at[1] for ref in refs], gs_ref)
    merge_stats(stat_ref, shift_ref, term_ref)
    acc_ref[...] = jnp.zeros(acc_ref.shape, F32)
    dqt_ref[...] = jnp.zeros(dqt_ref.shape, F32)
    edge, pair = z >> 1, z & 1

    def visit(group, half, part, mask):
        key_value = key_value_tile(kv_refs, half, part)
        key, value = key_value[:, :E], key_value[:, E:]
        for head in range(GROUP):
            cols = slice(head * HEAD_COLS, (head + 1) * HEAD_COLS)
            scores = dot(key, qs_ref[group, cols, :], 1, 1) * SCALE2
            dots = dot(value, gs_ref[group, cols, :], 1, 1)
            if mask is not None:
                scores = jnp.where(mask, scores, NEG)
            prob = jnp.exp2(scores - shift_ref[group, :, cols])
            prob_ref[:, cols] = prob.astype(BF16)
            slope_ref[:, cols] = (prob * (dots - term_ref[group, :, cols])).astype(BF16)
        slope = slope_ref[...]
        acc_ref[half, part, :, :E] += dot(slope, qs_ref[group], 1, 0)
        acc_ref[half, part, :, E:] += dot(prob_ref[...], gs_ref[group], 1, 0)
        dqt_ref[group] += dot(key, slope, 0, 0)

    @pl.loop(0, 2 * PARTS - 1, unroll=True)
    def _(index):
        visit(*free_visit(index, edge), None)

    for group in range(2):
        visit(group, group, edge, causal_mask(group, z, ring, core))

    scales = jnp.where(iota((1, 2 * E), 1) < E, SCALE, 1.0)
    for half in range(2):
        for part in range(PARTS):
            tile = (acc_ref[half, part] * scales).reshape(2, 2, HALF, 2 * E)
            rows = slice(half * HALF, (half + 1) * HALF)
            for piece in range(2):
                dkv0_ref[piece ^ pair, part, rows, :] = tile[0, piece]
                dkv1_ref[piece ^ pair, part, rows, :] = tile[1, piece].astype(BF16)
    targets = (dq0_ref, dq1_ref, dq2_ref, dq3_ref)
    for group in range(2):
        for head in range(GROUP):
            cols = slice(head * HEAD_COLS, (head + 1) * HEAD_COLS)
            turn_ref[...] = dqt_ref[group, :, cols].T * SCALE
            for ref, slot in zip(targets, slots):
                start = pl.multiple_of(slot * HALF, HALF)
                ref[group * HALF : (group + 1) * HALF, head * E : (head + 1) * E] = turn_ref[
                    pl.ds(start, HALF), :
                ].astype(ref.dtype)


def shape(dims, dtype):
    return jax.ShapeDtypeStruct(dims, dtype)


def swapped(x, axis):
    return lax.ppermute(x, axis, [(0, 1), (1, 0)])


def far_swapped(x):
    pairs = [(i, i ^ 5) for i in range(LINE)]
    return lax.ppermute(x, ("quad", "far"), pairs)


def from_ring(x, step):
    return lax.ppermute(x, "ring", [(i, (i + step) % TEAM) for i in range(TEAM)])


def per_device(queries, keys, values, cotangent, seg_lengths, seg_return, owner_slot, ref_term):
    head = lax.axis_index(("far_col", "near_col", "far"))
    place_names = (("quad", "pair"), "ring", "core", "far")
    where = jnp.stack([lax.axis_index(name) for name in place_names]).astype(I32)
    width = GROUP * E

    kv_own = jnp.concatenate(
        [jnp.broadcast_to(x[None], (LINE, ROWS, E)) for x in (keys, values)], axis=2
    )
    qg0, seg = call(
        pack_kernel,
        (shape((2, ROWS + 16, width), BF16), shape((8, E), F32)),
        scalars=1,
        inputs=5,
    )(
        where, queries, cotangent, owner_slot.reshape(1, ROWS),
        seg_lengths.reshape(1, E), seg_return.reshape(1, E),
    )
    from_far = far_swapped(ref_term)
    kv_own, from_far = lax.optimization_barrier((kv_own, from_far))
    lane = iota((8, E), 1) >> 4
    terms = jnp.where(lane == head, jnp.tile(ref_term, 8)[None], 0.0)
    terms = jnp.where(lane == (head ^ 1), jnp.tile(from_far, 8)[None], terms)
    kv0 = lax.all_to_all(kv_own, ("quad", "pair"), 0, 0, tiled=True)
    qg1, qg3 = from_ring(qg0, 1), from_ring(qg0, 3)
    terms = terms + swapped(terms, "near_col")
    qg1, terms = lax.optimization_barrier((qg1, terms))
    qg2 = from_ring(qg1, 1)
    terms = terms + swapped(terms, "far_col")
    kv0, terms, qg1, qg2, qg3 = lax.optimization_barrier((kv0, terms, qg1, qg2, qg3))
    team = (qg0, qg1, qg2, qg3)
    kv1 = swapped(kv0, "core")
    table = lax.all_to_all(
        jnp.broadcast_to(terms[None], (2 * LINE, 8, E)), ("quad", "pair", "core"), 0, 0, tiled=True
    )
    pairs = 9 * TILE * COLS
    kv_scratch = [pltpu.VMEM((2, COLS, E), BF16), pltpu.VMEM((2, COLS, E), BF16)]
    stat = call(
        forward_kernel,
        shape((8, COLS), F32),
        kv_scratch + [pltpu.VMEM((2, 8, COLS), F32)] * 3,
        scalars=1,
        inputs=6,
        cost=pl.CostEstimate(flops=4 * E * pairs, bytes_accessed=4 << 20, transcendentals=pairs),
    )(where, *team, kv0, kv1)
    stat = call(lookup_kernel, shape((TEAM, 8, COLS), F32), scalars=1, inputs=7)(
        where, *team, stat, table, seg
    )
    stats = lax.all_to_all(stat, "ring", 0, 0, tiled=True)
    core_grad = (2, LINE // 2, ROWS, 2 * E)
    query_grad = shape((ROWS, width), BF16)
    grad0, grad1, dq0, *dqs = call(
        backward_kernel,
        (
            shape(core_grad, F32), shape(core_grad, BF16), shape((ROWS, width), F32),
            query_grad, query_grad, query_grad,
        ),
        kv_scratch
        + [
            pltpu.VMEM((2, E, COLS), F32),
            pltpu.VMEM((2, PARTS, TILE, 2 * E), F32),
            pltpu.VMEM((2, 1, COLS), F32),
            pltpu.VMEM((2, 1, COLS), F32),
            pltpu.VMEM((TILE, COLS), BF16),
            pltpu.VMEM((TILE, COLS), BF16),
            pltpu.VMEM((HEAD_COLS, E), F32),
        ],
        scalars=1,
        inputs=7,
        cost=pl.CostEstimate(flops=10 * E * pairs, bytes_accessed=5 << 20, transcendentals=pairs),
    )(where, *team, kv0, kv1, stats)

    own = grad0 + swapped(grad1, "core").astype(F32)
    parts = (own[0] + swapped(own[1].astype(BF16), "pair").astype(F32)).astype(BF16)
    parts = lax.all_to_all(parts, "quad", 0, 0, tiled=True)
    kv_grad = jnp.sum(parts.astype(F32), axis=0).astype(BF16)

    for step, part in enumerate(dqs, 1):
        dq0 = dq0 + from_ring(part, TEAM - step).astype(F32)
    return dq0.astype(BF16), kv_grad[:, :E], kv_grad[:, E:]


def solution(mesh):
    fine = Mesh(
        mesh.devices.reshape(LINE // 2, 2, TEAM, 2, 2, 2, 2),
        ("quad", "pair", "ring", "core", "far_col", "near_col", "far"),
    )
    ctx = ("quad", "pair", "ring", "core")
    head = ("far_col", "near_col", "far")
    return jax.shard_map(
        per_device,
        mesh=fine,
        in_specs=(
            P(ctx, head), P(ctx, head), P(ctx, head), P(ctx, head),
            P(), P(), P(ctx), P(ctx + head),
        ),
        out_specs=(P(ctx, head), P(ctx, head), P(ctx, head)),
        check_vma=False,
    )
```
